256 devices in a mesh: batch: 4 (over y), seq: 64 (over x, z, core).
Axes of the slice: x: 4, y: 4, z: 8, core: 2. Of those that a mesh axis runs over, the one named last changes fastest.
Arguments:
- query: bfloat16 [4, 8192, 1024], P('batch', 'seq'), may hold values from -6 to 6
- key: bfloat16 [4, 8192, 1024], P('batch', 'seq'), may hold values from -6 to 6
- value: bfloat16 [4, 8192, 1024], P('batch', 'seq'), may hold values from -6 to 6
- grad_attn: bfloat16 [4, 8192, 1024], P('batch', 'seq'), may hold values from -6 to 6
- scale_ids: int32 [4, 8192], P('batch', 'seq'), may hold values from 0 to 12, never falling along the last dimension, each value on 1 to 3276 neighbouring positions
Outputs:
- attn_out: bfloat16 [4, 8192, 1024], P('batch', 'seq')
- query_grad: bfloat16 [4, 8192, 1024], P('batch', 'seq')
- key_grad: bfloat16 [4, 8192, 1024], P('batch', 'seq')
- value_grad: bfloat16 [4, 8192, 1024], P('batch', 'seq')
The draws below stay inside these ranges and needn't reach their ends.
Inputs may be any that keep to these rules, and one draw needn't show every extreme that they name: `scale_ids`: along each image's positions the scale id never falls; every id occurs; no scale has more than 3276 positions and one has exactly that many.
All inputs are finite; a program needn't handle non-finite values.
Results may differ from the reference program's by a relative error of at most 0.03.
Values may be sent and summed in bfloat16 or wider, within the bound.
No kernel may reach another device: no remote copies, remote signals or barrier semaphores. Data moves between devices by JAX's collectives and lax.ppermute only.
A program may use at most 128 MiB of HBM per device.

```python
import math
import jax
import jax.numpy as jnp
import numpy as np
from jax import lax

HEADS = 8
HDIM = 128
SCALES = 13
SEQ = 8192
IMAGES = 4
SCALE_MOST = 3276


def draw_query(key, part):
    key = jax.random.fold_in(key, 11)
    base = jnp.clip(jax.random.normal(key, (IMAGES, SEQ, HEADS * HDIM), jnp.float32), -6.0, 6.0)
    return base.astype(jnp.bfloat16)


def draw_key(key, part):
    key = jax.random.fold_in(key, 23)
    base = jnp.clip(jax.random.normal(key, (IMAGES, SEQ, HEADS * HDIM), jnp.float32), -6.0, 6.0)
    return base.astype(jnp.bfloat16)


def block_scale(rng, extent, pieces, smallest, high):
    def one(dim, shards_of):
        heights = jax.random.uniform(jax.random.fold_in(jax.random.fold_in(rng, 6), dim), (shards_of,), jnp.float32, smallest / len(pieces), high / len(pieces))
        return jnp.repeat(jnp.exp(heights), extent[dim] // shards_of).reshape((-1,) + (1,) * (len(extent) - dim - 1))

    loudness = one(*pieces[0])
    for cut in pieces[1:]:
        loudness = loudness * one(*cut)
    return loudness


def length_profile(number_of, total, reach, lean):
    portions = [(1 << 20) // math.isqrt(rank ** lean) + 1 for rank in range(2, number_of + 1)]
    surplus, counts = total - reach - (number_of - 1), [1] * (number_of - 1)
    while surplus > 0:
        movable = [i for i in range(number_of - 1) if counts[i] < reach]
        pool, remaining = sum([portions[i] for i in movable]), surplus
        for i in movable:
            more = min(reach - counts[i], max(1, remaining * portions[i] // pool), surplus)
            counts[i] = counts[i] + more
            surplus = surplus - more
    return np.array([reach] + counts)


def ragged_sizes(rng, amount, total, most, slope):
    if amount == 2:
        one = jax.random.randint(rng, (), max(1, total - most), min(most, total - 1) + 1)
        return jnp.stack([one, total - one])
    tallies = jnp.asarray(length_profile(amount, total, most, slope), jnp.int32)
    pairs = (amount - 1) // 2
    giver, receiver = tallies[1:1 + 2 * pairs:2], tallies[2:2 + 2 * pairs:2]
    margin = jnp.minimum(giver - 1, most - receiver)
    shifted = jax.random.randint(jax.random.fold_in(rng, 1), (pairs,), 0, 1 << 20) % (margin + 1)
    tallies = tallies.at[1:1 + 2 * pairs:2].set(giver - shifted).at[2:2 + 2 * pairs:2].set(receiver + shifted)
    return tallies[jax.random.permutation(jax.random.fold_in(rng, 2), amount)]


def noise(stream_key, extent, deviation, limit, split=(), kind=jnp.bfloat16):
    level = block_scale(stream_key, extent, split, -0.22, 0.18) if split else 1.0
    drawn = jax.random.normal(stream_key, extent, jnp.float32) * deviation * level
    return jnp.minimum(jnp.maximum(drawn, -limit), limit).astype(kind)


def setup_inputs(seed: int = 0) -> dict:
    seeds = jax.random.split(jax.random.key(seed), 6)
    return {
        "query": draw_query(jax.random.fold_in(seeds[5], 71), 0),
        "key": draw_key(jax.random.fold_in(seeds[5], 71), 0),
        "value": noise(seeds[2], (IMAGES, SEQ, HEADS * HDIM), 1.0, 6.0, ((0, 4), (1, 64))),
        "grad_attn": noise(seeds[3], (IMAGES, SEQ, HEADS * HDIM), 1.0, 6.0, ((0, 4), (1, 64))),
        "scale_ids": jax.vmap(lambda own: jnp.searchsorted(jnp.cumsum(ragged_sizes(own, SCALES, SEQ, SCALE_MOST, 2)), jnp.arange(SEQ), side="right"))(jax.random.split(seeds[4], IMAGES)).reshape((IMAGES, SEQ)).astype(jnp.int32),
    }


def reference(query, key, value, grad_attn, scale_ids):
    inv_root = HDIM ** -0.5
    outputs = []
    query_grads = []
    key_grads = []
    value_grads = []
    for image in range(IMAGES):
        allowed = scale_ids[image][None, :] <= scale_ids[image][:, None]

        def split_heads(arr):
            return arr.reshape(SEQ, HEADS, HDIM).transpose(1, 0, 2)

        def one_head(parts):
            q_head, k_head, v_head, do_head = parts
            scores = jnp.dot(q_head, k_head.T, preferred_element_type=jnp.float32) * inv_root
            scores = jnp.where(allowed, scores, -1e30)
            top = jnp.max(scores, axis=1, keepdims=True)
            lse = top + jnp.log(jnp.sum(jnp.exp(scores - top), axis=1, keepdims=True))
            probs = jnp.exp(scores - lse)
            weights = probs.astype(jnp.bfloat16)
            attn = jnp.dot(weights, v_head, preferred_element_type=jnp.float32).astype(jnp.bfloat16)
            delta = jnp.sum(do_head.astype(jnp.float32) * attn.astype(jnp.float32), axis=1, keepdims=True)
            dprobs = jnp.dot(do_head, v_head.T, preferred_element_type=jnp.float32)
            dscores = (probs * (dprobs - delta) * inv_root).astype(jnp.bfloat16)
            q_grad = jnp.dot(dscores, k_head, preferred_element_type=jnp.float32).astype(jnp.bfloat16)
            k_grad = jnp.dot(dscores.T, q_head, preferred_element_type=jnp.float32).astype(jnp.bfloat16)
            v_grad = jnp.dot(weights.T, do_head, preferred_element_type=jnp.float32).astype(jnp.bfloat16)
            return attn, q_grad, k_grad, v_grad

        attn, q_grad, k_grad, v_grad = lax.map(one_head, (split_heads(query[image]), split_heads(key[image]), split_heads(value[image]), split_heads(grad_attn[image])))

        def join_heads(arr):
            return arr.transpose(1, 0, 2).reshape(SEQ, HEADS * HDIM)

        outputs.append(join_heads(attn))
        query_grads.append(join_heads(q_grad))
        key_grads.append(join_heads(k_grad))
        value_grads.append(join_heads(v_grad))
    return (jnp.stack(outputs), jnp.stack(query_grads), jnp.stack(key_grads), jnp.stack(value_grads))
```

```python
import functools

import jax
import jax.numpy as jnp
from jax import lax
from jax.experimental import pallas as pl
from jax.experimental.pallas import tpu as pltpu
from jax.sharding import Mesh, PartitionSpec as P

HEADS = 8
HDIM = 128
ROWS = 128
TILE = 16
XS, ZS, CS = 4, 8, 2
CHUNKS = XS * ZS * CS
QB = 512
KB = 512
STEPS = CHUNKS * ROWS // KB
INV_ROOT = HDIM ** -0.5
LOG2E = 1.4426950408889634
NEG = -1e30

NT = (((1,), (1,)), ((), ()))
TN = (((0,), (0,)), ((), ()))


def dot(a, b, dims=(((1,), (0,)), ((), ()))):
    return lax.dot_general(a, b, dims, preferred_element_type=jnp.float32)


def lanes(fn, tile):
    return jnp.concatenate(
        [fn(i, tile[:, i * 128 : (i + 1) * 128]) for i in range(tile.shape[1] // 128)], axis=1
    )


PIECES = ((0, 0, 8), (3, 0, 8), (1, 0, 8), (2, 0, 4), (2, 4, 4))


def attention_kernel(at_ref, *refs):
    pieces, (qd_a, qd_b), refs = refs[:10], refs[10:12], refs[12:]
    (ad_a, ad_b), grads, refs = refs[:2], refs[2:10], refs[10:]
    kvs_ref, qd_ref, ad_ref, s_scr, e_scr, dk_scr, dv_scr, acc_scr, dq_scr, qs_scr, row_scr, sems, qsems = refs
    x, own_core = at_ref[0], at_ref[1]

    def first_chunk(distance, other):
        core = 1 - own_core if other else own_core
        return (lax.rem(x + distance, XS) * CS + core) * ZS

    copies = [
        pltpu.make_async_copy(qd_a, qd_ref.at[0:4], qsems.at[0]),
        pltpu.make_async_copy(qd_b, qd_ref.at[4:8], qsems.at[1]),
    ]
    for i, (distance, start, count) in enumerate(PIECES):
        for other in (0, 1):
            n = 2 * i + other
            copies.append(
                pltpu.make_async_copy(
                    pieces[n], kvs_ref.at[pl.ds(first_chunk(distance, other) + start, count)], sems.at[n]
                )
            )
    for copy in copies:
        copy.start()
    dk_scr[...] = jnp.zeros_like(dk_scr)
    dv_scr[...] = jnp.zeros_like(dv_scr)
    for copy in copies:
        copy.wait()

    key_scales = kvs_ref[:, 256:272, :].astype(jnp.float32)[:, 0, :]
    chunk = lax.broadcasted_iota(jnp.int32, key_scales.shape, 0)
    lane = lax.broadcasted_iota(jnp.int32, key_scales.shape, 1)
    core = (chunk // ZS) % CS
    parity = chunk % 2
    is_first = (core == 0) & (parity == 0) & (lane == 0)
    is_last = (core == 1) & (parity == 1) & (lane == ROWS - 1)

    def parts(step):
        base = (step // 4) * 16 + 2 * (step % 4)
        return (base, base + 8)

    def rows_of(base, start):
        return kvs_ref[pl.ds(base, 2), start : start + ROWS, :].reshape(2 * ROWS, HDIM)

    def both(step, start):
        a, b = parts(step)
        return jnp.concatenate([rows_of(a, start), rows_of(b, start)], axis=0)

    def one_block(block, _):
        first = block * (QB // ROWS)
        q = qd_ref[pl.ds(first, QB // ROWS), 0:128, :].reshape(QB, HDIM)
        do = qd_ref[pl.ds(first, QB // ROWS), 128:256, :].reshape(QB, HDIM)
        own = qd_ref[pl.ds(first, QB // ROWS), 256:272, :].astype(jnp.float32)[:, 0, :]
        for i in range(QB // ROWS):
            qs_scr[i * ROWS : (i + 1) * ROWS, :] = jnp.broadcast_to(own[i : i + 1, :], (ROWS, ROWS)).T
        low, high = jnp.min(own), jnp.max(own)
        n_steps = jnp.sum(jnp.where(is_first & (key_scales <= high), 1.0, 0.0)).astype(jnp.int32)
        n_full = jnp.sum(jnp.where(is_last & (key_scales <= low), 1.0, 0.0)).astype(jnp.int32)

        def scores(masked, step, _):
            s = dot(q, both(step, 0), NT)
            if masked:
                a, b = parts(step)
                ks = [
                    kvs_ref[c, 256:272, :].astype(jnp.float32)[0:1, :]
                    for c in (a, a + 1, b, b + 1)
                ]
                qs = qs_scr[...]
                s = lanes(lambda i, t: jnp.where(ks[i] <= qs, t, NEG), s)
            s_scr[step] = s
            top = row_scr[...]
            for i in range(KB // 128):
                top = jnp.maximum(top, s[:, i * 128 : (i + 1) * 128])
            row_scr[...] = top
            return 0

        row_scr[...] = jnp.full_like(row_scr, NEG)
        lax.fori_loop(0, n_full, functools.partial(scores, False), 0)
        lax.fori_loop(n_full, n_steps, functools.partial(scores, True), 0)
        top = jnp.max(row_scr[...], axis=1, keepdims=True) * (INV_ROOT * LOG2E)
        row_scr[...] = jnp.broadcast_to(top, row_scr.shape)
        acc_scr[...] = jnp.zeros_like(acc_scr)
        ones = jnp.ones((KB, HDIM), jnp.bfloat16)

        def forward(step, _):
            top = row_scr[...]
            e = lanes(lambda i, t: jnp.exp2(t * (INV_ROOT * LOG2E) - top).astype(jnp.bfloat16), s_scr[step])
            e_scr[step] = e
            acc_scr[...] += dot(e, jnp.concatenate([both(step, 128), ones], axis=1))
            return 0

        lax.fori_loop(0, n_steps, forward, 0)
        inv = 1.0 / acc_scr[:, 128:256]
        attn = acc_scr[:, 0:128] * inv
        for i in range(QB // ROWS):
            ad_ref[first + i, 0:128, :] = attn[i * ROWS : (i + 1) * ROWS, :].astype(jnp.bfloat16)
        do_n = (do.astype(jnp.float32) * inv).astype(jnp.bfloat16)
        delta = jnp.sum(do_n.astype(jnp.float32) * attn, axis=1, keepdims=True)
        row_scr[...] = jnp.broadcast_to(delta, row_scr.shape)
        dq_scr[...] = jnp.zeros_like(dq_scr)

        def backward(step, _):
            delta = row_scr[...]
            e = e_scr[step]
            k = both(step, 0)
            dp = dot(do_n, both(step, 128), NT)
            ds = lanes(
                lambda i, t: (e[:, i * 128 : (i + 1) * 128].astype(jnp.float32) * (t - delta)).astype(jnp.bfloat16),
                dp,
            )
            dq_scr[...] += dot(ds, k)
            dk = dot(ds, q, TN).reshape(4, ROWS, HDIM)
            dv = dot(e, do_n, TN).reshape(4, ROWS, HDIM)
            a, b = parts(step)
            dk_scr[pl.ds(a, 2)] += dk[0:2]
            dk_scr[pl.ds(b, 2)] += dk[2:4]
            dv_scr[pl.ds(a, 2)] += dv[0:2]
            dv_scr[pl.ds(b, 2)] += dv[2:4]
            return 0

        lax.fori_loop(0, n_steps, backward, 0)
        for i in range(QB // ROWS):
            ad_ref[first + i, 128:256, :] = (dq_scr[i * ROWS : (i + 1) * ROWS, :] * INV_ROOT).astype(jnp.bfloat16)
        return 0

    lax.fori_loop(0, ZS * ROWS // QB, one_block, 0)

    ad_a[...] = ad_ref[0:4]
    ad_b[...] = ad_ref[4:8]
    for distance in range(XS):
        for other in (0, 1):
            out = grads[2 * distance + other]
            base = first_chunk(distance, other)
            out[:, 0:128, :] = (dk_scr[pl.ds(base, ZS)] * INV_ROOT).astype(jnp.bfloat16)
            out[:, 128:256, :] = dv_scr[pl.ds(base, ZS)].astype(jnp.bfloat16)


def attention(at, pieces, qds):
    vmem = pl.BlockSpec(memory_space=pltpu.VMEM)
    anywhere = pl.BlockSpec(memory_space=pl.ANY)
    half = jax.ShapeDtypeStruct((ZS // 2, 2 * ROWS, HDIM), jnp.bfloat16)
    whole = jax.ShapeDtypeStruct((ZS, 2 * ROWS, HDIM), jnp.bfloat16)
    outs = (half,) * 2 + (whole,) * 8
    return pl.pallas_call(
        attention_kernel,
        out_shape=outs,
        in_specs=[pl.BlockSpec(memory_space=pltpu.SMEM)] + [anywhere] * 12,
        out_specs=(vmem,) * len(outs),
        scratch_shapes=[
            pltpu.VMEM((CHUNKS, 2 * ROWS + TILE, HDIM), jnp.bfloat16),
            pltpu.VMEM((ZS, 2 * ROWS + TILE, HDIM), jnp.bfloat16),
            pltpu.VMEM((ZS, 2 * ROWS, HDIM), jnp.bfloat16),
            pltpu.VMEM((STEPS, QB, KB), jnp.float32),
            pltpu.VMEM((STEPS, QB, KB), jnp.bfloat16),
            pltpu.VMEM((CHUNKS, ROWS, HDIM), jnp.float32),
            pltpu.VMEM((CHUNKS, ROWS, HDIM), jnp.float32),
            pltpu.VMEM((QB, 2 * HDIM), jnp.float32),
            pltpu.VMEM((QB, HDIM), jnp.float32),
            pltpu.VMEM((QB, HDIM), jnp.float32),
            pltpu.VMEM((QB, HDIM), jnp.float32),
            pltpu.SemaphoreType.DMA((10,)),
            pltpu.SemaphoreType.DMA((2,)),
        ],
        compiler_params=pltpu.CompilerParams(vmem_limit_bytes=56 * 1024 * 1024),
        cost_estimate=pl.CostEstimate(flops=8 * 10**9, bytes_accessed=10 * 2**20, transcendentals=5 * 10**6),
    )(at, *pieces, *qds)


def pack_kernel(a_ref, b_ref, scale_ref, out_ref):
    scales = jnp.broadcast_to(scale_ref[...].astype(jnp.float32), (TILE, ROWS)).astype(jnp.bfloat16)
    for h in range(HEADS):
        out_ref[h, 0:128, :] = a_ref[0, :, h * HDIM : (h + 1) * HDIM]
        out_ref[h, 128:256, :] = b_ref[0, :, h * HDIM : (h + 1) * HDIM]
        out_ref[h, 256:272, :] = scales


def pack(a, b, scale_ids):
    vmem = pl.BlockSpec(memory_space=pltpu.VMEM)
    return pl.pallas_call(
        pack_kernel,
        out_shape=jax.ShapeDtypeStruct((HEADS, 2 * ROWS + TILE, HDIM), jnp.bfloat16),
        in_specs=[vmem] * 3,
        out_specs=vmem,
    )(a, b, scale_ids)


def unpack_kernel(in_ref, a_ref, b_ref):
    for h in range(HEADS):
        a_ref[0, :, h * HDIM : (h + 1) * HDIM] = in_ref[h, 0:128, :]
        b_ref[0, :, h * HDIM : (h + 1) * HDIM] = in_ref[h, 128:256, :]


def unpack(arr):
    vmem = pl.BlockSpec(memory_space=pltpu.VMEM)
    rows = jax.ShapeDtypeStruct((1, ROWS, HEADS * HDIM), jnp.bfloat16)
    return pl.pallas_call(
        unpack_kernel, out_shape=(rows, rows), in_specs=[vmem], out_specs=(vmem, vmem)
    )(arr)


def add(*arrs):
    total = arrs[0].astype(jnp.float32)
    for arr in arrs[1:]:
        total = total + arr.astype(jnp.float32)
    return total.astype(jnp.bfloat16)


def local(query, key, value, grad_attn, scale_ids):
    def over_heads(arr):
        return lax.all_to_all(arr, "z", split_axis=0, concat_axis=0, tiled=True)

    def right(arr):
        return lax.ppermute(arr, "x", [(i, (i + 1) % XS) for i in range(XS)])

    def left(arr):
        return lax.ppermute(arr, "x", [(i, (i + XS - 1) % XS) for i in range(XS)])

    def mirror(arr):
        return lax.ppermute(arr, "x", [(i, XS - 1 - i) for i in range(XS)])

    def twin(arr):
        return lax.ppermute(arr, "core", [(0, 1), (1, 0)])

    half = ZS // 2
    at = jnp.stack([lax.axis_index("x"), lax.axis_index("core")]).astype(jnp.int32)

    kvs = over_heads(pack(key, value, scale_ids))
    from_left, from_right = right(kvs), left(kvs)
    qd = over_heads(pack(query, grad_attn, scale_ids))
    opposite_a, opposite_b = right(from_left[:half]), left(from_right[half:])
    qd_b = mirror(qd[half:])
    pieces = []
    for piece in (kvs, from_left, from_right, opposite_a, opposite_b):
        pieces += [piece, twin(piece)]

    ad_a, ad_b, *grads = attention(at, pieces, (qd[:half], qd_b))

    sums = [None] * XS
    for distance in (2, 1, 3, 0):
        sums[distance] = add(grads[2 * distance], twin(grads[2 * distance + 1]))
    from_a, from_b = right(sums[2][:half]), left(sums[2][half:])
    to_right = jnp.concatenate([add(sums[1][:half], from_a), sums[1][half:]], axis=0)
    to_left = jnp.concatenate([sums[3][:half], add(sums[3][half:], from_b)], axis=0)
    ad_back = over_heads(jnp.concatenate([ad_a, mirror(ad_b)], axis=0))
    dkv_back = over_heads(add(sums[0], right(to_right), left(to_left)))
    return unpack(ad_back) + unpack(dkv_back)


def solution(mesh):
    fine = Mesh(mesh.devices.reshape(mesh.devices.shape[0], XS, ZS, CS), ("batch", "x", "z", "core"))
    seq = ("x", "z", "core")
    rows = P("batch", seq, None)
    return jax.shard_map(
        local,
        mesh=fine,
        in_specs=(rows, rows, rows, rows, P("batch", seq)),
        out_specs=(rows, rows, rows, rows),
        check_vma=False,
    )
```

```python
import functools

import jax
import jax.numpy as jnp
from jax import lax
from jax.experimental import pallas as pl
from jax.experimental.pallas import tpu as pltpu
from jax.sharding import Mesh, PartitionSpec as P

HEADS = 8
HDIM = 128
ROWS = 128
TILE = 16
XS, ZS, CS = 4, 8, 2
CHUNKS = XS * ZS * CS
QB = 512
KB = 512
SLAB = 256
GROUP = 32
COLS = tuple(slice(i, i + SLAB) for i in range(0, QB, SLAB))
STEPS = CHUNKS * ROWS // KB
INV_ROOT = HDIM ** -0.5
LOG2E = 1.4426950408889634
NEG = -1e30

NT = (((1,), (1,)), ((), ()))
TN = (((0,), (0,)), ((), ()))


def dot(a, b, dims=(((1,), (0,)), ((), ()))):
    return lax.dot_general(a, b, dims, preferred_element_type=jnp.float32)


PIECES = ((0, 0, 8), (3, 0, 8), (1, 0, 8), (2, 0, 4), (2, 4, 4))


def attention_kernel(at_ref, *refs):
    pieces, qd_in, ad_ref, grads, refs = refs[:10], refs[10], refs[11], refs[12:20], refs[20:]
    kvs_ref, qd_ref, s_scr, e_scr, dk_scr, dv_scr, acc_scr, dq_scr, don_scr, q_scr, ds_scr, top_scr, sum_scr, qs_scr, sems, qsem = refs
    x, own_core = at_ref[0], at_ref[1]

    def first_chunk(distance, other):
        core = 1 - own_core if other else own_core
        return (lax.rem(x + distance, XS) * CS + core) * ZS

    copies = [pltpu.make_async_copy(qd_in, qd_ref, qsem.at[0])]
    for i, (distance, start, count) in enumerate(PIECES):
        for other in (0, 1):
            n = 2 * i + other
            copies.append(
                pltpu.make_async_copy(
                    pieces[n], kvs_ref.at[pl.ds(first_chunk(distance, other) + start, count)], sems.at[n]
                )
            )
    for copy in copies:
        copy.start()
    dk_scr[...] = jnp.zeros_like(dk_scr)
    dv_scr[...] = jnp.zeros_like(dv_scr)
    for copy in copies:
        copy.wait()

    key_scales = kvs_ref[:, 256:272, :].astype(jnp.float32)[:, 0, :]
    chunk = lax.broadcasted_iota(jnp.int32, key_scales.shape, 0)
    lane = lax.broadcasted_iota(jnp.int32, key_scales.shape, 1)
    core = (chunk // ZS) % CS
    parity = chunk % 2
    is_first = (core == 0) & (parity == 0) & (lane == 0)
    is_last = (core == 1) & (parity == 1) & (lane == ROWS - 1)

    def parts(step):
        base = (step // 4) * 16 + 2 * (step % 4)
        return (base, base + 8)

    def slab(step, half, start):
        return kvs_ref[pl.ds(parts(step)[half], 2), start : start + ROWS, :].reshape(SLAB, HDIM)

    def down(row):
        return jnp.broadcast_to(row, (ROWS, ROWS)).T

    def fold(tile, op):
        return op(tile.reshape(tile.shape[0] // 8, 8, tile.shape[1]), axis=0)

    def one_block(block, _):
        first = block * (QB // ROWS)

        def rows(start):
            return qd_ref[pl.ds(first, QB // ROWS), start : start + ROWS, :].reshape(QB, HDIM)

        own = qd_ref[pl.ds(first, QB // ROWS), 256:272, :].astype(jnp.float32)[:, 0, :]
        for i in range(QB // ROWS):
            qs_scr[:, i * ROWS : (i + 1) * ROWS] = jnp.broadcast_to(own[i : i + 1, :], (8, ROWS))
        low, high = jnp.min(own), jnp.max(own)
        n_steps = jnp.sum(jnp.where(is_first & (key_scales <= high), 1.0, 0.0)).astype(jnp.int32)
        n_full = jnp.sum(jnp.where(is_last & (key_scales <= low), 1.0, 0.0)).astype(jnp.int32)

        def scores(masked, step, _):
            for half in range(KB // SLAB):
                k = slab(step, half, 0)
                if masked:
                    ks = [
                        down(kvs_ref[parts(step)[half] + i, 256:272, :].astype(jnp.float32)[0:1, :])
                        for i in range(SLAB // ROWS)
                    ]
                for cols in COLS:
                    s = dot(k, q_scr[cols, :], NT)
                    top = top_scr[:, cols]
                    for r in range(0, SLAB, GROUP):
                        tile = s[r : r + GROUP, :]
                        if masked:
                            own_ks = ks[r // ROWS][r % ROWS : r % ROWS + GROUP, :]
                            tile = jnp.concatenate(
                                [
                                    jnp.where(
                                        own_ks <= qs_scr[0:1, cols.start + j : cols.start + j + ROWS],
                                        tile[:, j : j + ROWS],
                                        NEG,
                                    )
                                    for j in range(0, SLAB, ROWS)
                                ],
                                axis=1,
                            )
                        s_scr[step, half * SLAB + r : half * SLAB + r + GROUP, cols] = tile
                        top = jnp.maximum(top, fold(tile, jnp.max))
                    top_scr[:, cols] = top
            return 0

        q_scr[...] = rows(0)
        top_scr[...] = jnp.full_like(top_scr, NEG)
        lax.fori_loop(0, n_full, functools.partial(scores, False), 0)
        lax.fori_loop(n_full, n_steps, functools.partial(scores, True), 0)
        top = jnp.max(top_scr[...], axis=0, keepdims=True) * (INV_ROOT * LOG2E)
        top_scr[...] = jnp.broadcast_to(top, top_scr.shape)
        sum_scr[...] = jnp.zeros_like(sum_scr)
        acc_scr[...] = jnp.zeros_like(acc_scr)

        def forward(step, _):
            for half in range(KB // SLAB):
                total = sum_scr[...]
                for r in range(half * SLAB, (half + 1) * SLAB, GROUP):
                    e = jnp.exp2(s_scr[step, r : r + GROUP, :] * (INV_ROOT * LOG2E) - top_scr[0:1, :])
                    total = total + fold(e, jnp.sum)
                    e_scr[step, r : r + GROUP, :] = e.astype(jnp.bfloat16)
                sum_scr[...] = total
                acc_scr[...] += dot(slab(step, half, 128), e_scr[step, half * SLAB : (half + 1) * SLAB, :], TN)
            return 0

        lax.fori_loop(0, n_steps, forward, 0)
        inv = 1.0 / jnp.sum(sum_scr[...], axis=0, keepdims=True)
        attn = (acc_scr[...] * inv).T
        inv_rows = jnp.broadcast_to(inv, (HDIM, QB)).T
        for i in range(QB // ROWS):
            ad_ref[first + i, 0:128, :] = attn[i * ROWS : (i + 1) * ROWS, :].astype(jnp.bfloat16)
        do_n = (rows(128).astype(jnp.float32) * inv_rows).astype(jnp.bfloat16)
        don_scr[...] = do_n
        delta = jnp.sum(do_n.astype(jnp.float32) * attn, axis=1, keepdims=True)
        top_scr[...] = jnp.broadcast_to(delta, (QB, HDIM)).T[0:8, :]
        dq_scr[...] = jnp.zeros_like(dq_scr)

        def backward(step, _):
            for half in range(KB // SLAB):
                own = slice(half * SLAB, (half + 1) * SLAB)
                v = slab(step, half, 128)
                for cols in COLS:
                    dp = dot(v, don_scr[cols, :], NT)
                    for r in range(0, SLAB, GROUP):
                        e = e_scr[step, half * SLAB + r : half * SLAB + r + GROUP, cols].astype(jnp.float32)
                        ds = e * (dp[r : r + GROUP, :] - top_scr[0:1, cols])
                        ds_scr[half, r : r + GROUP, cols] = ds.astype(jnp.bfloat16)
                dv = dot(e_scr[step, own, :], don_scr[...])
                dk = dot(ds_scr[half], q_scr[...])
                at_chunks = pl.ds(parts(step)[half], 2)
                dv_scr[at_chunks] += dv.reshape(2, ROWS, HDIM)
                dk_scr[at_chunks] += dk.reshape(2, ROWS, HDIM)
                dq_scr[...] += dot(slab(step, half, 0), ds_scr[half], TN)
            return 0

        lax.fori_loop(0, n_steps, backward, 0)
        dq = (dq_scr[...] * INV_ROOT).T.astype(jnp.bfloat16)
        for i in range(QB // ROWS):
            ad_ref[first + i, 128:256, :] = dq[i * ROWS : (i + 1) * ROWS, :]
        return 0

    lax.fori_loop(0, ZS * ROWS // QB, one_block, 0)

    for distance in range(XS):
        for other in (0, 1):
            out = grads[2 * distance + other]
            base = first_chunk(distance, other)
            out[:, 0:128, :] = (dk_scr[pl.ds(base, ZS)] * INV_ROOT).astype(jnp.bfloat16)
            out[:, 128:256, :] = dv_scr[pl.ds(base, ZS)].astype(jnp.bfloat16)


def attention(at, pieces, qd):
    vmem = pl.BlockSpec(memory_space=pltpu.VMEM)
    outs = (jax.ShapeDtypeStruct((ZS, 2 * ROWS, HDIM), jnp.bfloat16),) * 9
    return pl.pallas_call(
        attention_kernel,
        out_shape=outs,
        in_specs=[pl.BlockSpec(memory_space=pltpu.SMEM)] + [vmem] * 11,
        out_specs=(vmem,) * len(outs),
        scratch_shapes=[
            pltpu.VMEM((CHUNKS, 2 * ROWS + TILE, HDIM), jnp.bfloat16),
            pltpu.VMEM((ZS, 2 * ROWS + TILE, HDIM), jnp.bfloat16),
            pltpu.VMEM((STEPS, KB, QB), jnp.float32),
            pltpu.VMEM((STEPS, KB, QB), jnp.bfloat16),
            pltpu.VMEM((CHUNKS, ROWS, HDIM), jnp.float32),
            pltpu.VMEM((CHUNKS, ROWS, HDIM), jnp.float32),
            pltpu.VMEM((HDIM, QB), jnp.float32),
            pltpu.VMEM((HDIM, QB), jnp.float32),
            pltpu.VMEM((QB, HDIM), jnp.bfloat16),
            pltpu.VMEM((QB, HDIM), jnp.bfloat16),
            pltpu.VMEM((KB // SLAB, SLAB, QB), jnp.bfloat16),
            pltpu.VMEM((8, QB), jnp.float32),
            pltpu.VMEM((8, QB), jnp.float32),
            pltpu.VMEM((8, QB), jnp.float32),
            pltpu.SemaphoreType.DMA((10,)),
            pltpu.SemaphoreType.DMA((1,)),
        ],
        compiler_params=pltpu.CompilerParams(vmem_limit_bytes=42 * 1024 * 1024),
        cost_estimate=pl.CostEstimate(flops=8 * 10**9, bytes_accessed=10 * 2**20, transcendentals=5 * 10**6),
    )(at, *pieces, qd)


def pack_kernel(a_ref, b_ref, scale_ref, out_ref):
    scales = jnp.broadcast_to(scale_ref[...].astype(jnp.float32), (TILE, ROWS)).astype(jnp.bfloat16)
    for h in range(HEADS):
        out_ref[h, 0:128, :] = a_ref[0, :, h * HDIM : (h + 1) * HDIM]
        out_ref[h, 128:256, :] = b_ref[0, :, h * HDIM : (h + 1) * HDIM]
        out_ref[h, 256:272, :] = scales


def pack(a, b, scale_ids):
    vmem = pl.BlockSpec(memory_space=pltpu.VMEM)
    return pl.pallas_call(
        pack_kernel,
        out_shape=jax.ShapeDtypeStruct((HEADS, 2 * ROWS + TILE, HDIM), jnp.bfloat16),
        in_specs=[vmem] * 3,
        out_specs=vmem,
    )(a, b, scale_ids)


def unpack_kernel(in_ref, *outs):
    for h in range(HEADS):
        for i, out in enumerate(outs):
            out[0, :, h * HDIM : (h + 1) * HDIM] = in_ref[h, i * ROWS : (i + 1) * ROWS, :]


def unpack(arr):
    vmem = pl.BlockSpec(memory_space=pltpu.VMEM)
    rows = jax.ShapeDtypeStruct((1, ROWS, HEADS * HDIM), jnp.bfloat16)
    n = arr.shape[1] // ROWS
    return pl.pallas_call(unpack_kernel, out_shape=(rows,) * n, in_specs=[vmem], out_specs=(vmem,) * n)(arr)


def add(*arrs):
    total = arrs[0].astype(jnp.float32)
    for arr in arrs[1:]:
        total = total + arr.astype(jnp.float32)
    return total.astype(jnp.bfloat16)


def local(query, key, value, grad_attn, scale_ids):
    def over_heads(arr):
        return lax.all_to_all(arr, "z", split_axis=0, concat_axis=0, tiled=True)

    def right(arr):
        return lax.ppermute(arr, "x", [(i, (i + 1) % XS) for i in range(XS)])

    def left(arr):
        return lax.ppermute(arr, "x", [(i, (i + XS - 1) % XS) for i in range(XS)])

    def swap(arr):
        pairs = [
            (x * ZS + z, (XS - 1 - x if z >= ZS // 2 else x) * ZS + z) for x in range(XS) for z in range(ZS)
        ]
        return lax.ppermute(arr, ("x", "z"), pairs)

    def twin(arr):
        return lax.ppermute(arr, "core", [(0, 1), (1, 0)])

    half = ZS // 2
    at = jnp.stack([lax.axis_index("x"), lax.axis_index("core")]).astype(jnp.int32)

    kvs = over_heads(pack(key, value, scale_ids))
    swapped = swap(pack(query, grad_attn, scale_ids))
    kvs, swapped = lax.optimization_barrier((kvs, swapped))
    from_left, from_right = right(kvs), left(kvs)
    qd = over_heads(swapped)
    opposite_a, opposite_b = right(from_left[:half]), left(from_right[half:])
    pieces = []
    for piece in (kvs, from_left, from_right, opposite_a, opposite_b):
        pieces += [piece, twin(piece)]

    ad, *grads = attention(at, pieces, qd)

    far = add(grads[4], twin(grads[5]))
    far, *grads = lax.optimization_barrier((far, *grads))
    sums = {distance: add(grads[2 * distance], twin(grads[2 * distance + 1])) for distance in (3, 1, 0)}
    ad, sums[1], sums[3] = lax.optimization_barrier((ad, sums[1], sums[3]))
    ad_back = over_heads(ad)
    k, v = slice(0, ROWS), slice(ROWS, 2 * ROWS)
    key_left = left(sums[3][:, k])
    key_right = right(add(sums[1][:, k], right(far[:, k])))
    value_left = left(add(sums[3][:, v], left(far[:, v])))
    value_right = right(sums[1][:, v])
    key_sum = add(sums[0][:, k], key_right, key_left)
    value_sum = add(sums[0][:, v], value_right, value_left)
    value_sum, ad_back = lax.optimization_barrier((value_sum, ad_back))
    return (
        *unpack(swap(ad_back)),
        *unpack(over_heads(key_sum)),
        *unpack(over_heads(value_sum)),
    )


def solution(mesh):
    fine = Mesh(mesh.devices.reshape(mesh.devices.shape[0], XS, ZS, CS), ("batch", "x", "z", "core"))
    seq = ("x", "z", "core")
    rows = P("batch", seq, None)
    return jax.shard_map(
        local,
        mesh=fine,
        in_specs=(rows, rows, rows, rows, P("batch", seq)),
        out_specs=(rows, rows, rows, rows),
        check_vma=False,
    )
```

```python
import functools

import jax
import jax.numpy as jnp
from jax import lax
from jax.experimental import pallas as pl
from jax.experimental.pallas import tpu as pltpu
from jax.sharding import Mesh, PartitionSpec as P

HEADS = 8
HDIM = 128
ROWS = 128
TILE = 16
XS, ZS, CS = 4, 8, 2
CHUNKS = XS * ZS * CS
QB = 512
KB = 512
SLAB = 256
GROUP = 32
COLS = tuple(slice(i, i + SLAB) for i in range(0, QB, SLAB))
STEPS = CHUNKS * ROWS // KB
INV_ROOT = HDIM ** -0.5
LOG2E = 1.4426950408889634
NEG = -1e30

NT = (((1,), (1,)), ((), ()))
TN = (((0,), (0,)), ((), ()))


def dot(a, b, dims=(((1,), (0,)), ((), ()))):
    return lax.dot_general(a, b, dims, preferred_element_type=jnp.float32)


PIECES = ((0, 0, 8), (3, 0, 8), (1, 0, 8), (2, 0, 4), (2, 4, 4))
N_PIECES = 2 * len(PIECES)


def attention_kernel(at_ref, *refs):
    pieces, qd_in, ad_ref, grads, refs = (
        refs[:N_PIECES], refs[N_PIECES], refs[N_PIECES + 1], refs[N_PIECES + 2 : N_PIECES + 10], refs[N_PIECES + 10 :],
    )
    kvs_ref, qd_ref, s_scr, e_scr, dk_scr, dv_scr, acc_scr, dq_scr, don_scr, q_scr, ds_scr, now_scr, dp_scr, top_scr, tops_scr, delta_scr, sum_scr, qs_scr, sems, qsem = refs
    x, own_core = at_ref[0], at_ref[1]

    def first_chunk(distance, other):
        core = 1 - own_core if other else own_core
        return (lax.rem(x + distance, XS) * CS + core) * ZS

    copies = [pltpu.make_async_copy(qd_in, qd_ref, qsem.at[0])]
    for i, (distance, start, count) in enumerate(PIECES):
        for other in (0, 1):
            n = 2 * i + other
            copies.append(
                pltpu.make_async_copy(
                    pieces[n], kvs_ref.at[pl.ds(first_chunk(distance, other) + start, count)], sems.at[n]
                )
            )
    for copy in copies:
        copy.start()
    dk_scr[...] = jnp.zeros_like(dk_scr)
    dv_scr[...] = jnp.zeros_like(dv_scr)
    for copy in copies:
        copy.wait()

    key_scales = kvs_ref[:, 256:272, :].astype(jnp.float32)[:, 0, :]
    chunk = lax.broadcasted_iota(jnp.int32, key_scales.shape, 0)
    lane = lax.broadcasted_iota(jnp.int32, key_scales.shape, 1)
    core = (chunk // ZS) % CS
    parity = chunk % 2
    is_first = (core == 0) & (parity == 0) & (lane == 0)
    is_last = (core == 1) & (parity == 1) & (lane == ROWS - 1)

    def parts(step):
        base = (step // 4) * 16 + 2 * (step % 4)
        return (base, base + 8)

    def slab(step, half, start):
        return kvs_ref[pl.ds(parts(step)[half], 2), start : start + ROWS, :].reshape(SLAB, HDIM)

    def down(row):
        return jnp.broadcast_to(row, (ROWS, ROWS)).T

    def fold(tile, op):
        return op(tile.reshape(tile.shape[0] // 8, 8, tile.shape[1]), axis=0)

    def one_block(block, _):
        first = block * (QB // ROWS)

        def rows(start):
            return qd_ref[pl.ds(first, QB // ROWS), start : start + ROWS, :].reshape(QB, HDIM)

        own = qd_ref[pl.ds(first, QB // ROWS), 256:272, :].astype(jnp.float32)[:, 0, :]
        for i in range(QB // ROWS):
            qs_scr[:, i * ROWS : (i + 1) * ROWS] = jnp.broadcast_to(own[i : i + 1, :], (8, ROWS))
        low, high = jnp.min(own), jnp.max(own)
        n_steps = jnp.sum(jnp.where(is_first & (key_scales <= high), 1.0, 0.0)).astype(jnp.int32)
        n_steps = jnp.maximum(n_steps, 2)
        n_full = jnp.sum(jnp.where(is_last & (key_scales <= low), 1.0, 0.0)).astype(jnp.int32)

        def scores(masked, step):
            for half in range(KB // SLAB):
                k = slab(step, half, 0)
                if masked:
                    ks = [
                        down(kvs_ref[parts(step)[half] + i, 256:272, :].astype(jnp.float32)[0:1, :])
                        for i in range(SLAB // ROWS)
                    ]
                for cols in COLS:
                    s = dot(k, q_scr[cols, :], NT)
                    for r in range(0, SLAB, GROUP):
                        tile = s[r : r + GROUP, :]
                        if masked:
                            own_ks = ks[r // ROWS][r % ROWS : r % ROWS + GROUP, :]
                            tile = jnp.concatenate(
                                [
                                    jnp.where(
                                        own_ks <= qs_scr[0:1, cols.start + j : cols.start + j + ROWS],
                                        tile[:, j : j + ROWS],
                                        NEG,
                                    )
                                    for j in range(0, SLAB, ROWS)
                                ],
                                axis=1,
                            )
                        s_scr[half * SLAB + r : half * SLAB + r + GROUP, cols] = tile

        q_scr[...] = rows(0)
        top_scr[...] = jnp.full_like(top_scr, NEG)
        sum_scr[...] = jnp.zeros_like(sum_scr)
        acc_scr[...] = jnp.zeros_like(acc_scr)

        def weigh(step):
            for half in range(KB // SLAB):
                own = slice(half * SLAB, (half + 1) * SLAB)
                acc_scr[...] += dot(slab(step, half, 128), now_scr[own, :], TN)

        def exponentials(step):
            top = fold(s_scr[0:GROUP, :], jnp.max)
            for r in range(GROUP, KB, GROUP):
                top = jnp.maximum(top, fold(s_scr[r : r + GROUP, :], jnp.max))
            top = jnp.ceil(jnp.max(top, axis=0, keepdims=True) * (INV_ROOT * LOG2E))
            top = jnp.maximum(top_scr[0:1, :], top)
            drop = jnp.exp2(top_scr[0:1, :] - top)
            top_scr[...] = jnp.broadcast_to(top, top_scr.shape)
            tops_scr[step] = jnp.broadcast_to(top, top_scr.shape)
            acc_scr[...] = acc_scr[...] * drop
            total = sum_scr[...] * drop
            for r in range(0, KB, GROUP):
                e = jnp.exp2(s_scr[r : r + GROUP, :] * (INV_ROOT * LOG2E) - top)
                total = total + fold(e, jnp.sum)
                e = e.astype(jnp.bfloat16)
                now_scr[r : r + GROUP, :] = e
                e_scr[step, r : r + GROUP, :] = e
            sum_scr[...] = total

        def forward(masked, step, _):
            weigh(step - 1)
            exponentials(step)
            scores(masked, step + 1)
            return 0

        scores(True, 0)
        exponentials(0)
        scores(True, 1)
        n_open = jnp.maximum(n_full - 1, 1)
        lax.fori_loop(1, n_open, functools.partial(forward, False), 0)
        lax.fori_loop(n_open, n_steps - 1, functools.partial(forward, True), 0)
        weigh(n_steps - 2)
        exponentials(n_steps - 1)
        weigh(n_steps - 1)
        inv = 1.0 / jnp.sum(sum_scr[...], axis=0, keepdims=True)
        attn = (acc_scr[...] * inv).T
        inv_rows = jnp.broadcast_to(inv, (HDIM, QB)).T
        for i in range(QB // ROWS):
            ad_ref[first + i, 0:128, :] = attn[i * ROWS : (i + 1) * ROWS, :].astype(jnp.bfloat16)
        do_n = (rows(128).astype(jnp.float32) * inv_rows).astype(jnp.bfloat16)
        don_scr[...] = do_n
        delta = jnp.sum(do_n.astype(jnp.float32) * attn, axis=1, keepdims=True)
        delta_scr[...] = jnp.broadcast_to(delta, (QB, HDIM)).T[0:8, :]
        dq_scr[...] = jnp.zeros_like(dq_scr)

        def dprobs(step):
            for half in range(KB // SLAB):
                v = slab(step, half, 128)
                for cols in COLS:
                    dp_scr[half * SLAB : (half + 1) * SLAB, cols] = dot(v, don_scr[cols, :], NT)

        def backward(step, _):
            drop = jnp.exp2(tops_scr[step, 0:1, :] - top_scr[0:1, :])
            delta = delta_scr[0:1, :]
            for r in range(0, KB, GROUP):
                e = e_scr[step, r : r + GROUP, :].astype(jnp.float32) * drop
                now_scr[r : r + GROUP, :] = e.astype(jnp.bfloat16)
                ds_scr[r : r + GROUP, :] = (e * (dp_scr[r : r + GROUP, :] - delta)).astype(jnp.bfloat16)
            for half in range(KB // SLAB):
                dv = dot(now_scr[half * SLAB : (half + 1) * SLAB, :], don_scr[...])
                dv_scr[pl.ds(parts(step)[half], 2)] += dv.reshape(2, ROWS, HDIM)
            dprobs(jnp.minimum(step + 1, STEPS - 1))
            for half in range(KB // SLAB):
                own = slice(half * SLAB, (half + 1) * SLAB)
                dk_scr[pl.ds(parts(step)[half], 2)] += dot(ds_scr[own, :], q_scr[...]).reshape(2, ROWS, HDIM)
                dq_scr[...] += dot(slab(step, half, 0), ds_scr[own, :], TN)
            return 0

        dprobs(0)
        lax.fori_loop(0, n_steps, backward, 0)
        dq = (dq_scr[...] * INV_ROOT).T.astype(jnp.bfloat16)
        for i in range(QB // ROWS):
            ad_ref[first + i, 128:256, :] = dq[i * ROWS : (i + 1) * ROWS, :]
        return 0

    lax.fori_loop(0, ZS * ROWS // QB, one_block, 0)

    for distance in range(XS):
        for other in (0, 1):
            out = grads[2 * distance + other]
            base = first_chunk(distance, other)
            out[:, 0:128, :] = (dk_scr[pl.ds(base, ZS)] * INV_ROOT).astype(jnp.bfloat16)
            out[:, 128:256, :] = dv_scr[pl.ds(base, ZS)].astype(jnp.bfloat16)


def attention(at, pieces, qd):
    vmem = pl.BlockSpec(memory_space=pltpu.VMEM)
    outs = (jax.ShapeDtypeStruct((ZS, 2 * ROWS, HDIM), jnp.bfloat16),) * 9
    return pl.pallas_call(
        attention_kernel,
        out_shape=outs,
        in_specs=[pl.BlockSpec(memory_space=pltpu.SMEM)] + [vmem] * (N_PIECES + 1),
        out_specs=(vmem,) * len(outs),
        scratch_shapes=[
            pltpu.VMEM((CHUNKS, 2 * ROWS + TILE, HDIM), jnp.bfloat16),
            pltpu.VMEM((ZS, 2 * ROWS + TILE, HDIM), jnp.bfloat16),
            pltpu.VMEM((KB, QB), jnp.float32),
            pltpu.VMEM((STEPS, KB, QB), jnp.bfloat16),
            pltpu.VMEM((CHUNKS, ROWS, HDIM), jnp.float32),
            pltpu.VMEM((CHUNKS, ROWS, HDIM), jnp.float32),
            pltpu.VMEM((HDIM, QB), jnp.float32),
            pltpu.VMEM((HDIM, QB), jnp.float32),
            pltpu.VMEM((QB, HDIM), jnp.bfloat16),
            pltpu.VMEM((QB, HDIM), jnp.bfloat16),
            pltpu.VMEM((KB, QB), jnp.bfloat16),
            pltpu.VMEM((KB, QB), jnp.bfloat16),
            pltpu.VMEM((KB, QB), jnp.float32),
            pltpu.VMEM((8, QB), jnp.float32),
            pltpu.VMEM((STEPS, 8, QB), jnp.float32),
            pltpu.VMEM((8, QB), jnp.float32),
            pltpu.VMEM((8, QB), jnp.float32),
            pltpu.VMEM((8, QB), jnp.float32),
            pltpu.SemaphoreType.DMA((N_PIECES,)),
            pltpu.SemaphoreType.DMA((1,)),
        ],
        compiler_params=pltpu.CompilerParams(vmem_limit_bytes=38 * 1024 * 1024),
        cost_estimate=pl.CostEstimate(flops=8 * 10**9, bytes_accessed=10 * 2**20, transcendentals=5 * 10**6),
    )(at, *pieces, qd)


def pack_kernel(a_ref, b_ref, scale_ref, out_ref):
    scales = jnp.broadcast_to(scale_ref[...].astype(jnp.float32), (TILE, ROWS)).astype(jnp.bfloat16)
    for h in range(HEADS):
        out_ref[h, 0:128, :] = a_ref[0, :, h * HDIM : (h + 1) * HDIM]
        out_ref[h, 128:256, :] = b_ref[0, :, h * HDIM : (h + 1) * HDIM]
        out_ref[h, 256:272, :] = scales


def pack(a, b, scale_ids):
    vmem = pl.BlockSpec(memory_space=pltpu.VMEM)
    return pl.pallas_call(
        pack_kernel,
        out_shape=jax.ShapeDtypeStruct((HEADS, 2 * ROWS + TILE, HDIM), jnp.bfloat16),
        in_specs=[vmem] * 3,
        out_specs=vmem,
    )(a, b, scale_ids)


def unpack_kernel(in_ref, *outs):
    for h in range(HEADS):
        for i, out in enumerate(outs):
            out[0, :, h * HDIM : (h + 1) * HDIM] = in_ref[h, i * ROWS : (i + 1) * ROWS, :]


def unpack(arr):
    vmem = pl.BlockSpec(memory_space=pltpu.VMEM)
    rows = jax.ShapeDtypeStruct((1, ROWS, HEADS * HDIM), jnp.bfloat16)
    n = arr.shape[1] // ROWS
    return pl.pallas_call(unpack_kernel, out_shape=(rows,) * n, in_specs=[vmem], out_specs=(vmem,) * n)(arr)


def add(*arrs):
    total = arrs[0].astype(jnp.float32)
    for arr in arrs[1:]:
        total = total + arr.astype(jnp.float32)
    return total.astype(jnp.bfloat16)


def local(query, key, value, grad_attn, scale_ids):
    def over_heads(arr):
        return lax.all_to_all(arr, "z", split_axis=0, concat_axis=0, tiled=True)

    def right(arr):
        return lax.ppermute(arr, "x", [(i, (i + 1) % XS) for i in range(XS)])

    def left(arr):
        return lax.ppermute(arr, "x", [(i, (i + XS - 1) % XS) for i in range(XS)])

    def swap(arr):
        pairs = [
            (x * ZS + z, (XS - 1 - x if z >= ZS // 2 else x) * ZS + z) for x in range(XS) for z in range(ZS)
        ]
        return lax.ppermute(arr, ("x", "z"), pairs)

    def twin(arr):
        return lax.ppermute(arr, "core", [(0, 1), (1, 0)])

    half = ZS // 2
    at = jnp.stack([lax.axis_index("x"), lax.axis_index("core")]).astype(jnp.int32)

    kvs = over_heads(pack(key, value, scale_ids))
    swapped = swap(pack(query, grad_attn, scale_ids))
    kvs, swapped = lax.optimization_barrier((kvs, swapped))
    from_left, from_right = right(kvs), left(kvs)
    qd = over_heads(swapped)
    opposite_a, opposite_b = right(from_left[:half]), left(from_right[half:])
    pieces = []
    for piece in (kvs, from_left, from_right, opposite_a, opposite_b):
        pieces += [piece, twin(piece)]

    ad, *grads = attention(at, pieces, qd)

    far = add(grads[4], twin(grads[5]))
    far, *grads = lax.optimization_barrier((far, *grads))
    sums = {distance: add(grads[2 * distance], twin(grads[2 * distance + 1])) for distance in (3, 1, 0)}
    k, v = slice(0, ROWS), slice(ROWS, 2 * ROWS)
    key_left = left(sums[3][:, k])
    key_relay = add(sums[1][:, k], right(far[:, k]))
    value_relay = add(sums[3][:, v], left(far[:, v]))
    ad, key_relay, value_relay = lax.optimization_barrier((ad, key_relay, value_relay))
    ad_back = over_heads(ad)
    key_right, value_left = right(key_relay), left(value_relay)
    value_right = right(sums[1][:, v])
    key_sum = add(sums[0][:, k], key_right, key_left)
    value_sum = add(sums[0][:, v], value_right, value_left)
    sums = jnp.concatenate([key_sum, value_sum], axis=1)
    sums, ad_back = lax.optimization_barrier((sums, ad_back))
    return (*unpack(swap(ad_back)), *unpack(over_heads(sums)))


def solution(mesh):
    fine = Mesh(mesh.devices.reshape(mesh.devices.shape[0], XS, ZS, CS), ("batch", "x", "z", "core"))
    seq = ("x", "z", "core")
    rows = P("batch", seq, None)
    return jax.shard_map(
        local,
        mesh=fine,
        in_specs=(rows, rows, rows, rows, P("batch", seq)),
        out_specs=(rows, rows, rows, rows),
        check_vma=False,
    )
```

```python
import functools

import jax
import jax.numpy as jnp
from jax import lax
from jax.experimental import pallas as pl
from jax.experimental.pallas import tpu as pltpu
from jax.sharding import Mesh, PartitionSpec as P

HEADS = 8
HDIM = 128
ROWS = 128
TILE = 16
XS, ZS, CS = 4, 8, 2
CHUNKS = XS * ZS * CS
QB = 512
KB = 512
SLAB = 256
GROUP = 32
COLS = tuple(slice(i, i + SLAB) for i in range(0, QB, SLAB))
STEPS = CHUNKS * ROWS // KB
INV_ROOT = HDIM ** -0.5
LOG2E = 1.4426950408889634
NEG = -1e30

NT = (((1,), (1,)), ((), ()))
TN = (((0,), (0,)), ((), ()))


def dot(a, b, dims=(((1,), (0,)), ((), ()))):
    return lax.dot_general(a, b, dims, preferred_element_type=jnp.float32)


PIECES = (
    (0, 0, 8), (3, 0, 4), (3, 4, 4), (1, 0, 4), (1, 4, 4), (2, 0, 4), (2, 4, 4)
)
N_PIECES = 2 * len(PIECES)


def attention_kernel(at_ref, *refs):
    pieces, qd_in, ad_ref, grads, refs = (
        refs[:N_PIECES], refs[N_PIECES], refs[N_PIECES + 1], refs[N_PIECES + 2 : N_PIECES + 10], refs[N_PIECES + 10 :],
    )
    kvs_ref, qd_ref, s_scr, e_scr, dk_scr, dv_scr, acc_scr, dq_scr, don_scr, dont_scr, q_scr, qt_scr, ds_scr, now_scr, dp_scr, top_scr, tops_scr, delta_scr, sum_scr, qs_scr, sems, qsem = refs
    x, own_core = at_ref[0], at_ref[1]

    def first_chunk(distance, other):
        core = 1 - own_core if other else own_core
        return (lax.rem(x + distance, XS) * CS + core) * ZS

    copies = [pltpu.make_async_copy(qd_in, qd_ref, qsem.at[0])]
    for i, (distance, start, count) in enumerate(PIECES):
        for other in (0, 1):
            n = 2 * i + other
            copies.append(
                pltpu.make_async_copy(
                    pieces[n], kvs_ref.at[pl.ds(first_chunk(distance, other) + start, count)], sems.at[n]
                )
            )
    for copy in copies:
        copy.start()
    dk_scr[...] = jnp.zeros_like(dk_scr)
    dv_scr[...] = jnp.zeros_like(dv_scr)
    for copy in copies:
        copy.wait()

    key_scales = kvs_ref[:, 256:272, :].astype(jnp.float32)[:, 0, :]
    chunk = lax.broadcasted_iota(jnp.int32, key_scales.shape, 0)
    lane = lax.broadcasted_iota(jnp.int32, key_scales.shape, 1)
    core = (chunk // ZS) % CS
    parity = chunk % 2
    is_first = (core == 0) & (parity == 0) & (lane == 0)
    is_last = (core == 1) & (parity == 1) & (lane == ROWS - 1)

    def parts(step):
        base = (step // 4) * 16 + 2 * (step % 4)
        return (base, base + 8)

    def slab(step, half, start):
        return kvs_ref[pl.ds(parts(step)[half], 2), start : start + ROWS, :].reshape(SLAB, HDIM)

    def down(row):
        return jnp.broadcast_to(row, (ROWS, ROWS)).T

    def fold(tile, op):
        return op(tile.reshape(tile.shape[0] // 8, 8, tile.shape[1]), axis=0)

    def one_block(block, _):
        first = block * (QB // ROWS)

        def rows(start):
            return qd_ref[pl.ds(first, QB // ROWS), start : start + ROWS, :].reshape(QB, HDIM)

        own = qd_ref[pl.ds(first, QB // ROWS), 256:272, :].astype(jnp.float32)[:, 0, :]
        for i in range(QB // ROWS):
            qs_scr[:, i * ROWS : (i + 1) * ROWS] = jnp.broadcast_to(own[i : i + 1, :], (8, ROWS))
        low, high = jnp.min(own), jnp.max(own)
        n_steps = jnp.sum(jnp.where(is_first & (key_scales <= high), 1.0, 0.0)).astype(jnp.int32)
        n_steps = jnp.maximum(n_steps, 2)
        n_full = jnp.sum(jnp.where(is_last & (key_scales <= low), 1.0, 0.0)).astype(jnp.int32)

        def scores(masked, step):
            for half in range(KB // SLAB):
                k = slab(step, half, 0)
                if masked:
                    ks = [
                        down(kvs_ref[parts(step)[half] + i, 256:272, :].astype(jnp.float32)[0:1, :])
                        for i in range(SLAB // ROWS)
                    ]
                for cols in COLS:
                    s = dot(k, q_scr[cols, :], NT)
                    for r in range(0, SLAB, GROUP):
                        tile = s[r : r + GROUP, :]
                        if masked:
                            own_ks = ks[r // ROWS][r % ROWS : r % ROWS + GROUP, :]
                            tile = jnp.concatenate(
                                [
                                    jnp.where(
                                        own_ks <= qs_scr[0:1, cols.start + j : cols.start + j + ROWS],
                                        tile[:, j : j + ROWS],
                                        NEG,
                                    )
                                    for j in range(0, SLAB, ROWS)
                                ],
                                axis=1,
                            )
                        s_scr[half * SLAB + r : half * SLAB + r + GROUP, cols] = tile

        q_scr[...] = rows(0)
        qt_scr[...] = rows(0).astype(jnp.float32).T.astype(jnp.bfloat16)
        top_scr[...] = jnp.full_like(top_scr, NEG)
        sum_scr[...] = jnp.zeros_like(sum_scr)
        acc_scr[...] = jnp.zeros_like(acc_scr)

        def weigh(step):
            for half in range(KB // SLAB):
                own = slice(half * SLAB, (half + 1) * SLAB)
                acc_scr[...] += dot(slab(step, half, 128), now_scr[own, :], TN)

        def exponentials(step):
            top = fold(s_scr[0:GROUP, :], jnp.max)
            for r in range(GROUP, KB, GROUP):
                top = jnp.maximum(top, fold(s_scr[r : r + GROUP, :], jnp.max))
            top = jnp.ceil(jnp.max(top, axis=0, keepdims=True) * (INV_ROOT * LOG2E))
            top = jnp.maximum(top_scr[0:1, :], top)
            drop = jnp.exp2(top_scr[0:1, :] - top)
            top_scr[...] = jnp.broadcast_to(top, top_scr.shape)
            tops_scr[step] = jnp.broadcast_to(top, top_scr.shape)
            acc_scr[...] = acc_scr[...] * drop
            total = sum_scr[...] * drop
            for r in range(0, KB, GROUP):
                e = jnp.exp2(s_scr[r : r + GROUP, :] * (INV_ROOT * LOG2E) - top)
                total = total + fold(e, jnp.sum)
                e = e.astype(jnp.bfloat16)
                now_scr[r : r + GROUP, :] = e
                e_scr[step, r : r + GROUP, :] = e
            sum_scr[...] = total

        def forward(masked, step, _):
            weigh(step - 1)
            exponentials(step)
            scores(masked, step + 1)
            return 0

        scores(True, 0)
        exponentials(0)
        scores(True, 1)
        n_open = jnp.maximum(n_full - 1, 1)
        lax.fori_loop(1, n_open, functools.partial(forward, False), 0)
        lax.fori_loop(n_open, n_steps - 1, functools.partial(forward, True), 0)
        weigh(n_steps - 2)
        exponentials(n_steps - 1)
        weigh(n_steps - 1)
        inv = 1.0 / jnp.sum(sum_scr[...], axis=0, keepdims=True)
        attn = (acc_scr[...] * inv).T
        inv_rows = jnp.broadcast_to(inv, (HDIM, QB)).T
        for i in range(QB // ROWS):
            ad_ref[first + i, 0:128, :] = attn[i * ROWS : (i + 1) * ROWS, :].astype(jnp.bfloat16)
        do_n = (rows(128).astype(jnp.float32) * inv_rows).astype(jnp.bfloat16)
        don_scr[...] = do_n
        dont_scr[...] = do_n.astype(jnp.float32).T.astype(jnp.bfloat16)
        delta = jnp.sum(do_n.astype(jnp.float32) * attn, axis=1, keepdims=True)
        delta_scr[...] = jnp.broadcast_to(delta, (QB, HDIM)).T[0:8, :]
        dq_scr[...] = jnp.zeros_like(dq_scr)

        def dprobs(step):
            for half in range(KB // SLAB):
                v = slab(step, half, 128)
                for cols in COLS:
                    dp_scr[half * SLAB : (half + 1) * SLAB, cols] = dot(v, don_scr[cols, :], NT)

        def backward(step, _):
            drop = jnp.exp2(tops_scr[step, 0:1, :] - top_scr[0:1, :])
            delta = delta_scr[0:1, :]
            for r in range(0, KB, GROUP):
                e = e_scr[step, r : r + GROUP, :].astype(jnp.float32) * drop
                now_scr[r : r + GROUP, :] = e.astype(jnp.bfloat16)
                ds_scr[r : r + GROUP, :] = (e * (dp_scr[r : r + GROUP, :] - delta)).astype(jnp.bfloat16)
            for half in range(KB // SLAB):
                dv = dot(dont_scr[...], now_scr[half * SLAB : (half + 1) * SLAB, :], NT)
                for i in range(SLAB // ROWS):
                    dv_scr[parts(step)[half] + i] += dv[:, i * ROWS : (i + 1) * ROWS]
            dprobs(jnp.minimum(step + 1, STEPS - 1))
            for half in range(KB // SLAB):
                own = slice(half * SLAB, (half + 1) * SLAB)
                dk = dot(qt_scr[...], ds_scr[own, :], NT)
                for i in range(SLAB // ROWS):
                    dk_scr[parts(step)[half] + i] += dk[:, i * ROWS : (i + 1) * ROWS]
                dq_scr[...] += dot(slab(step, half, 0), ds_scr[own, :], TN)
            return 0

        dprobs(0)
        lax.fori_loop(0, n_steps, backward, 0)
        dq = (dq_scr[...] * INV_ROOT).T.astype(jnp.bfloat16)
        for i in range(QB // ROWS):
            ad_ref[first + i, 128:256, :] = dq[i * ROWS : (i + 1) * ROWS, :]
        return 0

    lax.fori_loop(0, ZS * ROWS // QB, one_block, 0)

    for distance in range(XS):
        for other in (0, 1):
            out = grads[2 * distance + other]
            base = first_chunk(distance, other)
            out[:, 0:128, :] = (dk_scr[pl.ds(base, ZS)] * INV_ROOT).astype(jnp.bfloat16)
            out[:, 128:256, :] = dv_scr[pl.ds(base, ZS)].astype(jnp.bfloat16)


def attention(at, pieces, qd):
    vmem = pl.BlockSpec(memory_space=pltpu.VMEM)
    outs = (jax.ShapeDtypeStruct((ZS, 2 * ROWS, HDIM), jnp.bfloat16),) * 9
    return pl.pallas_call(
        attention_kernel,
        out_shape=outs,
        in_specs=[pl.BlockSpec(memory_space=pltpu.SMEM)] + [vmem] * (N_PIECES + 1),
        out_specs=(vmem,) * len(outs),
        scratch_shapes=[
            pltpu.VMEM((CHUNKS, 2 * ROWS + TILE, HDIM), jnp.bfloat16),
            pltpu.VMEM((ZS, 2 * ROWS + TILE, HDIM), jnp.bfloat16),
            pltpu.VMEM((KB, QB), jnp.float32),
            pltpu.VMEM((STEPS, KB, QB), jnp.bfloat16),
            pltpu.VMEM((CHUNKS, ROWS, HDIM), jnp.float32),
            pltpu.VMEM((CHUNKS, ROWS, HDIM), jnp.float32),
            pltpu.VMEM((HDIM, QB), jnp.float32),
            pltpu.VMEM((HDIM, QB), jnp.float32),
            pltpu.VMEM((QB, HDIM), jnp.bfloat16),
            pltpu.VMEM((HDIM, QB), jnp.bfloat16),
            pltpu.VMEM((QB, HDIM), jnp.bfloat16),
            pltpu.VMEM((HDIM, QB), jnp.bfloat16),
            pltpu.VMEM((KB, QB), jnp.bfloat16),
            pltpu.VMEM((KB, QB), jnp.bfloat16),
            pltpu.VMEM((KB, QB), jnp.float32),
            pltpu.VMEM((8, QB), jnp.float32),
            pltpu.VMEM((STEPS, 8, QB), jnp.float32),
            pltpu.VMEM((8, QB), jnp.float32),
            pltpu.VMEM((8, QB), jnp.float32),
            pltpu.VMEM((8, QB), jnp.float32),
            pltpu.SemaphoreType.DMA((N_PIECES,)),
            pltpu.SemaphoreType.DMA((1,)),
        ],
        compiler_params=pltpu.CompilerParams(vmem_limit_bytes=38 * 1024 * 1024),
        cost_estimate=pl.CostEstimate(flops=8 * 10**9, bytes_accessed=10 * 2**20, transcendentals=5 * 10**6),
    )(at, *pieces, qd)


def pack_kernel(a_ref, b_ref, scale_ref, out_ref):
    scales = jnp.broadcast_to(scale_ref[...].astype(jnp.float32), (TILE, ROWS)).astype(jnp.bfloat16)
    for h in range(HEADS):
        out_ref[h, 0:128, :] = a_ref[0, :, h * HDIM : (h + 1) * HDIM]
        out_ref[h, 128:256, :] = b_ref[0, :, h * HDIM : (h + 1) * HDIM]
        out_ref[h, 256:272, :] = scales


def pack(a, b, scale_ids):
    vmem = pl.BlockSpec(memory_space=pltpu.VMEM)
    return pl.pallas_call(
        pack_kernel,
        out_shape=jax.ShapeDtypeStruct((HEADS, 2 * ROWS + TILE, HDIM), jnp.bfloat16),
        in_specs=[vmem] * 3,
        out_specs=vmem,
    )(a, b, scale_ids)


def unpack_kernel(in_ref, *outs, turned):
    for h in range(HEADS):
        for i, out in enumerate(outs):
            tile = in_ref[h, i * ROWS : (i + 1) * ROWS, :]
            if turned:
                tile = tile.astype(jnp.float32).T.astype(jnp.bfloat16)
            out[0, :, h * HDIM : (h + 1) * HDIM] = tile


def unpack(arr, turned=False):
    vmem = pl.BlockSpec(memory_space=pltpu.VMEM)
    rows = jax.ShapeDtypeStruct((1, ROWS, HEADS * HDIM), jnp.bfloat16)
    n = arr.shape[1] // ROWS
    kernel = functools.partial(unpack_kernel, turned=turned)
    return pl.pallas_call(kernel, out_shape=(rows,) * n, in_specs=[vmem], out_specs=(vmem,) * n)(arr)


def add(*arrs):
    total = arrs[0].astype(jnp.float32)
    for arr in arrs[1:]:
        total = total + arr.astype(jnp.float32)
    return total.astype(jnp.bfloat16)


def local(query, key, value, grad_attn, scale_ids):
    def over_heads(arr):
        return lax.all_to_all(arr, "z", split_axis=0, concat_axis=0, tiled=True)

    def right(arr):
        return lax.ppermute(arr, "x", [(i, (i + 1) % XS) for i in range(XS)])

    def left(arr):
        return lax.ppermute(arr, "x", [(i, (i + XS - 1) % XS) for i in range(XS)])

    def swap(arr):
        pairs = [
            (x * ZS + z, (XS - 1 - x if z >= ZS // 2 else x) * ZS + z) for x in range(XS) for z in range(ZS)
        ]
        return lax.ppermute(arr, ("x", "z"), pairs)

    def twin(arr):
        return lax.ppermute(arr, "core", [(0, 1), (1, 0)])

    half = ZS // 2
    at = jnp.stack([lax.axis_index("x"), lax.axis_index("core")]).astype(jnp.int32)

    kvs = over_heads(pack(key, value, scale_ids))
    swapped = swap(pack(query, grad_attn, scale_ids))
    kvs, swapped = lax.optimization_barrier((kvs, swapped))
    kvs_twin = twin(kvs)
    low, high = kvs[:half], kvs[half:]
    left_low, right_high = right(low), left(high)
    left_high, right_low = right(high), left(low)
    swapped, kvs_twin = lax.optimization_barrier((swapped, kvs_twin))
    qd = over_heads(swapped)
    opposite_low, opposite_high = right(left_low), left(right_high)
    pieces = [kvs, kvs_twin]
    for piece in (left_low, left_high, right_low, right_high, opposite_low, opposite_high):
        pieces += [piece, twin(piece)]

    ad, *grads = attention(at, pieces, qd)

    k, v = slice(0, ROWS), slice(ROWS, 2 * ROWS)
    far = add(grads[4], twin(grads[5]))
    far, *grads = lax.optimization_barrier((far, *grads))
    sums = {distance: add(grads[2 * distance], twin(grads[2 * distance + 1])) for distance in (3, 1, 0)}
    key_left, value_right = left(sums[3][:, k]), right(sums[1][:, v])
    key_right = right(add(sums[1][:, k], right(far[:, k])))
    value_left = left(add(sums[3][:, v], left(far[:, v])))
    ad, key_left, value_right = lax.optimization_barrier((ad, key_left, value_right))
    ad_back = over_heads(ad)
    key_sum = add(sums[0][:, k], key_right, key_left)
    value_sum = add(sums[0][:, v], value_right, value_left)
    sums = jnp.concatenate([key_sum, value_sum], axis=1)
    sums, ad_back = lax.optimization_barrier((sums, ad_back))
    return (*unpack(swap(ad_back)), *unpack(over_heads(sums), turned=True))


def solution(mesh):
    fine = Mesh(mesh.devices.reshape(mesh.devices.shape[0], XS, ZS, CS), ("batch", "x", "z", "core"))
    seq = ("x", "z", "core")
    rows = P("batch", seq, None)
    return jax.shard_map(
        local,
        mesh=fine,
        in_specs=(rows, rows, rows, rows, P("batch", seq)),
        out_specs=(rows, rows, rows, rows),
        check_vma=False,
    )
```

```python
import functools

import jax
import jax.numpy as jnp
from jax import lax
from jax.experimental import pallas as pl
from jax.experimental.pallas import tpu as pltpu
from jax.sharding import Mesh, PartitionSpec as P

HEADS = 8
HDIM = 128
ROWS = 128
TILE = 16
XS, ZS, CS = 4, 8, 2
CHUNKS = XS * ZS * CS
QB = 512
KB = 512
SLAB = 256
GROUP = 32
COLS = tuple(slice(i, i + SLAB) for i in range(0, QB, SLAB))
STEPS = CHUNKS * ROWS // KB
INV_ROOT = HDIM ** -0.5
LOG2E = 1.4426950408889634
NEG = -1e30

NT = (((1,), (1,)), ((), ()))
TN = (((0,), (0,)), ((), ()))


def dot(a, b, dims=(((1,), (0,)), ((), ()))):
    return lax.dot_general(a, b, dims, preferred_element_type=jnp.float32)


PIECES = ((0, 0, 8), (3, 0, 8), (1, 0, 8), (2, 0, 4), (2, 4, 4))
N_PIECES = 2 * len(PIECES)


def attention_kernel(at_ref, *refs):
    pieces, qd_in, ad_ref, grads, refs = (
        refs[:N_PIECES], refs[N_PIECES], refs[N_PIECES + 1], refs[N_PIECES + 2 : N_PIECES + 10], refs[N_PIECES + 10 :],
    )
    kvs_ref, qd_ref, s_scr, e_scr, dk_scr, dv_scr, acc_scr, dq_scr, don_scr, dont_scr, q_scr, qt_scr, ds_scr, now_scr, dp_scr, top_scr, tops_scr, delta_scr, sum_scr, qs_scr, sems, qsem = refs
    x, own_core = at_ref[0], at_ref[1]

    def first_chunk(distance, other):
        core = 1 - own_core if other else own_core
        return (lax.rem(x + distance, XS) * CS + core) * ZS

    copies = [pltpu.make_async_copy(qd_in, qd_ref, qsem.at[0])]
    for i, (distance, start, count) in enumerate(PIECES):
        for other in (0, 1):
            n = 2 * i + other
            copies.append(
                pltpu.make_async_copy(
                    pieces[n], kvs_ref.at[pl.ds(first_chunk(distance, other) + start, count)], sems.at[n]
                )
            )
    for copy in copies:
        copy.start()
    dk_scr[...] = jnp.zeros_like(dk_scr)
    dv_scr[...] = jnp.zeros_like(dv_scr)
    for copy in copies:
        copy.wait()

    key_scales = kvs_ref[:, 256:272, :].astype(jnp.float32)[:, 0, :]
    chunk = lax.broadcasted_iota(jnp.int32, key_scales.shape, 0)
    lane = lax.broadcasted_iota(jnp.int32, key_scales.shape, 1)
    core = (chunk // ZS) % CS
    parity = chunk % 2
    is_first = (core == 0) & (parity == 0) & (lane == 0)
    is_last = (core == 1) & (parity == 1) & (lane == ROWS - 1)

    def parts(step):
        base = (step // 4) * 16 + 2 * (step % 4)
        return (base, base + 8)

    def slab(step, half, start):
        return kvs_ref[pl.ds(parts(step)[half], 2), start : start + ROWS, :].reshape(SLAB, HDIM)

    def down(row):
        return jnp.broadcast_to(row, (ROWS, ROWS)).T

    def fold(tile, op):
        return op(tile.reshape(tile.shape[0] // 8, 8, tile.shape[1]), axis=0)

    def one_block(block, _):
        first = block * (QB // ROWS)

        def rows(start):
            return qd_ref[pl.ds(first, QB // ROWS), start : start + ROWS, :].reshape(QB, HDIM)

        own = qd_ref[pl.ds(first, QB // ROWS), 256:272, :].astype(jnp.float32)[:, 0, :]
        for i in range(QB // ROWS):
            qs_scr[:, i * ROWS : (i + 1) * ROWS] = jnp.broadcast_to(own[i : i + 1, :], (8, ROWS))
        low, high = jnp.min(own), jnp.max(own)
        n_steps = jnp.sum(jnp.where(is_first & (key_scales <= high), 1.0, 0.0)).astype(jnp.int32)
        n_steps = jnp.maximum(n_steps, 2)
        n_full = jnp.sum(jnp.where(is_last & (key_scales <= low), 1.0, 0.0)).astype(jnp.int32)

        def scores(masked, step):
            for half in range(KB // SLAB):
                k = slab(step, half, 0)
                if masked:
                    ks = [
                        down(kvs_ref[parts(step)[half] + i, 256:272, :].astype(jnp.float32)[0:1, :])
                        for i in range(SLAB // ROWS)
                    ]
                for cols in COLS:
                    s = dot(k, q_scr[cols, :], NT)
                    for r in range(0, SLAB, GROUP):
                        tile = s[r : r + GROUP, :]
                        if masked:
                            own_ks = ks[r // ROWS][r % ROWS : r % ROWS + GROUP, :]
                            tile = jnp.concatenate(
                                [
                                    jnp.where(
                                        own_ks <= qs_scr[0:1, cols.start + j : cols.start + j + ROWS],
                                        tile[:, j : j + ROWS],
                                        NEG,
                                    )
                                    for j in range(0, SLAB, ROWS)
                                ],
                                axis=1,
                            )
                        s_scr[half * SLAB + r : half * SLAB + r + GROUP, cols] = tile

        q_scr[...] = rows(0)
        qt_scr[...] = rows(0).astype(jnp.float32).T.astype(jnp.bfloat16)
        top_scr[...] = jnp.full_like(top_scr, NEG)
        sum_scr[...] = jnp.zeros_like(sum_scr)
        acc_scr[...] = jnp.zeros_like(acc_scr)

        def weigh(step):
            for half in range(KB // SLAB):
                own = slice(half * SLAB, (half + 1) * SLAB)
                acc_scr[...] += dot(slab(step, half, 128), now_scr[own, :], TN)

        def exponentials(step):
            top = fold(s_scr[0:GROUP, :], jnp.max)
            for r in range(GROUP, KB, GROUP):
                top = jnp.maximum(top, fold(s_scr[r : r + GROUP, :], jnp.max))
            top = jnp.ceil(jnp.max(top, axis=0, keepdims=True) * (INV_ROOT * LOG2E))
            top = jnp.maximum(top_scr[0:1, :], top)
            drop = jnp.exp2(top_scr[0:1, :] - top)
            top_scr[...] = jnp.broadcast_to(top, top_scr.shape)
            tops_scr[step] = jnp.broadcast_to(top, top_scr.shape)
            acc_scr[...] = acc_scr[...] * drop
            total = sum_scr[...] * drop
            for r in range(0, KB, GROUP):
                e = jnp.exp2(s_scr[r : r + GROUP, :] * (INV_ROOT * LOG2E) - top)
                total = total + fold(e, jnp.sum)
                e = e.astype(jnp.bfloat16)
                now_scr[r : r + GROUP, :] = e
                e_scr[step, r : r + GROUP, :] = e
            sum_scr[...] = total

        def forward(masked, step, _):
            weigh(step - 1)
            exponentials(step)
            scores(masked, step + 1)
            return 0

        scores(True, 0)
        exponentials(0)
        scores(True, 1)
        n_open = jnp.maximum(n_full - 1, 1)
        lax.fori_loop(1, n_open, functools.partial(forward, False), 0)
        lax.fori_loop(n_open, n_steps - 1, functools.partial(forward, True), 0)
        weigh(n_steps - 2)
        exponentials(n_steps - 1)
        weigh(n_steps - 1)
        inv = 1.0 / jnp.sum(sum_scr[...], axis=0, keepdims=True)
        attn = (acc_scr[...] * inv).T
        inv_rows = jnp.broadcast_to(inv, (HDIM, QB)).T
        for i in range(QB // ROWS):
            ad_ref[first + i, 0:128, :] = attn[i * ROWS : (i + 1) * ROWS, :].astype(jnp.bfloat16)
        do_n = (rows(128).astype(jnp.float32) * inv_rows).astype(jnp.bfloat16)
        don_scr[...] = do_n
        dont_scr[...] = do_n.astype(jnp.float32).T.astype(jnp.bfloat16)
        delta = jnp.sum(do_n.astype(jnp.float32) * attn, axis=1, keepdims=True)
        delta_scr[...] = jnp.broadcast_to(delta, (QB, HDIM)).T[0:8, :]
        dq_scr[...] = jnp.zeros_like(dq_scr)

        def dprobs(step):
            for half in range(KB // SLAB):
                v = slab(step, half, 128)
                for cols in COLS:
                    dp_scr[half * SLAB : (half + 1) * SLAB, cols] = dot(v, don_scr[cols, :], NT)

        def backward(step, _):
            drop = jnp.exp2(tops_scr[step, 0:1, :] - top_scr[0:1, :])
            delta = delta_scr[0:1, :]
            for r in range(0, KB, GROUP):
                e = e_scr[step, r : r + GROUP, :].astype(jnp.float32) * drop
                now_scr[r : r + GROUP, :] = e.astype(jnp.bfloat16)
                ds_scr[r : r + GROUP, :] = (e * (dp_scr[r : r + GROUP, :] - delta)).astype(jnp.bfloat16)
            for half in range(KB // SLAB):
                dv = dot(dont_scr[...], now_scr[half * SLAB : (half + 1) * SLAB, :], NT)
                for i in range(SLAB // ROWS):
                    dv_scr[parts(step)[half] + i] += dv[:, i * ROWS : (i + 1) * ROWS]
            dprobs(jnp.minimum(step + 1, STEPS - 1))
            for half in range(KB // SLAB):
                own = slice(half * SLAB, (half + 1) * SLAB)
                dk = dot(qt_scr[...], ds_scr[own, :], NT)
                for i in range(SLAB // ROWS):
                    dk_scr[parts(step)[half] + i] += dk[:, i * ROWS : (i + 1) * ROWS]
                dq_scr[...] += dot(slab(step, half, 0), ds_scr[own, :], TN)
            return 0

        dprobs(0)
        lax.fori_loop(0, n_steps, backward, 0)
        dq = (dq_scr[...] * INV_ROOT).T.astype(jnp.bfloat16)
        for i in range(QB // ROWS):
            ad_ref[first + i, 128:256, :] = dq[i * ROWS : (i + 1) * ROWS, :]
        return 0

    lax.fori_loop(0, ZS * ROWS // QB, one_block, 0)

    for distance in range(XS):
        for other in (0, 1):
            out = grads[2 * distance + other]
            base = first_chunk(distance, other)
            out[:, 0:128, :] = (dk_scr[pl.ds(base, ZS)] * INV_ROOT).astype(jnp.bfloat16)
            out[:, 128:256, :] = dv_scr[pl.ds(base, ZS)].astype(jnp.bfloat16)


def attention(at, pieces, qd):
    vmem = pl.BlockSpec(memory_space=pltpu.VMEM)
    outs = (jax.ShapeDtypeStruct((ZS, 2 * ROWS, HDIM), jnp.bfloat16),) * 9
    return pl.pallas_call(
        attention_kernel,
        out_shape=outs,
        in_specs=[pl.BlockSpec(memory_space=pltpu.SMEM)] + [vmem] * (N_PIECES + 1),
        out_specs=(vmem,) * len(outs),
        scratch_shapes=[
            pltpu.VMEM((CHUNKS, 2 * ROWS + TILE, HDIM), jnp.bfloat16),
            pltpu.VMEM((ZS, 2 * ROWS + TILE, HDIM), jnp.bfloat16),
            pltpu.VMEM((KB, QB), jnp.float32),
            pltpu.VMEM((STEPS, KB, QB), jnp.bfloat16),
            pltpu.VMEM((CHUNKS, ROWS, HDIM), jnp.float32),
            pltpu.VMEM((CHUNKS, ROWS, HDIM), jnp.float32),
            pltpu.VMEM((HDIM, QB), jnp.float32),
            pltpu.VMEM((HDIM, QB), jnp.float32),
            pltpu.VMEM((QB, HDIM), jnp.bfloat16),
            pltpu.VMEM((HDIM, QB), jnp.bfloat16),
            pltpu.VMEM((QB, HDIM), jnp.bfloat16),
            pltpu.VMEM((HDIM, QB), jnp.bfloat16),
            pltpu.VMEM((KB, QB), jnp.bfloat16),
            pltpu.VMEM((KB, QB), jnp.bfloat16),
            pltpu.VMEM((KB, QB), jnp.float32),
            pltpu.VMEM((8, QB), jnp.float32),
            pltpu.VMEM((STEPS, 8, QB), jnp.float32),
            pltpu.VMEM((8, QB), jnp.float32),
            pltpu.VMEM((8, QB), jnp.float32),
            pltpu.VMEM((8, QB), jnp.float32),
            pltpu.SemaphoreType.DMA((N_PIECES,)),
            pltpu.SemaphoreType.DMA((1,)),
        ],
        compiler_params=pltpu.CompilerParams(vmem_limit_bytes=38 * 1024 * 1024),
        cost_estimate=pl.CostEstimate(flops=8 * 10**9, bytes_accessed=10 * 2**20, transcendentals=5 * 10**6),
    )(at, *pieces, qd)


def pack_kernel(a_ref, b_ref, scale_ref, out_ref):
    scales = jnp.broadcast_to(scale_ref[...].astype(jnp.float32), (TILE, ROWS)).astype(jnp.bfloat16)
    for h in range(HEADS):
        out_ref[h, 0:128, :] = a_ref[0, :, h * HDIM : (h + 1) * HDIM]
        out_ref[h, 128:256, :] = b_ref[0, :, h * HDIM : (h + 1) * HDIM]
        out_ref[h, 256:272, :] = scales


def pack(a, b, scale_ids):
    vmem = pl.BlockSpec(memory_space=pltpu.VMEM)
    return pl.pallas_call(
        pack_kernel,
        out_shape=jax.ShapeDtypeStruct((HEADS, 2 * ROWS + TILE, HDIM), jnp.bfloat16),
        in_specs=[vmem] * 3,
        out_specs=vmem,
    )(a, b, scale_ids)


def unpack_kernel(in_ref, *outs, turned):
    for h in range(HEADS):
        for i, out in enumerate(outs):
            tile = in_ref[h, i * ROWS : (i + 1) * ROWS, :]
            if turned:
                tile = tile.astype(jnp.float32).T.astype(jnp.bfloat16)
            out[0, :, h * HDIM : (h + 1) * HDIM] = tile


def unpack(arr, turned=False):
    vmem = pl.BlockSpec(memory_space=pltpu.VMEM)
    rows = jax.ShapeDtypeStruct((1, ROWS, HEADS * HDIM), jnp.bfloat16)
    n = arr.shape[1] // ROWS
    kernel = functools.partial(unpack_kernel, turned=turned)
    return pl.pallas_call(kernel, out_shape=(rows,) * n, in_specs=[vmem], out_specs=(vmem,) * n)(arr)


def add(*arrs):
    total = arrs[0].astype(jnp.float32)
    for arr in arrs[1:]:
        total = total + arr.astype(jnp.float32)
    return total.astype(jnp.bfloat16)


def local(query, key, value, grad_attn, scale_ids):
    def over_heads(arr):
        return lax.all_to_all(arr, "z", split_axis=0, concat_axis=0, tiled=True)

    def right(arr):
        return lax.ppermute(arr, "x", [(i, (i + 1) % XS) for i in range(XS)])

    def left(arr):
        return lax.ppermute(arr, "x", [(i, (i + XS - 1) % XS) for i in range(XS)])

    def swap(arr):
        pairs = [
            (x * ZS + z, (XS - 1 - x if z >= ZS // 2 else x) * ZS + z) for x in range(XS) for z in range(ZS)
        ]
        return lax.ppermute(arr, ("x", "z"), pairs)

    def twin(arr):
        return lax.ppermute(arr, "core", [(0, 1), (1, 0)])

    half = ZS // 2
    at = jnp.stack([lax.axis_index("x"), lax.axis_index("core")]).astype(jnp.int32)

    kvs = over_heads(pack(key, value, scale_ids))
    swapped = swap(pack(query, grad_attn, scale_ids))
    kvs, swapped = lax.optimization_barrier((kvs, swapped))
    from_left, from_right = right(kvs), left(kvs)
    qd = over_heads(swapped)
    opposite_a, opposite_b = right(from_left[:half]), left(from_right[half:])
    pieces = []
    for piece in (kvs, from_left, from_right, opposite_a, opposite_b):
        pieces += [piece, twin(piece)]

    ad, *grads = attention(at, pieces, qd)

    ad_back = over_heads(ad)
    far = add(grads[4], twin(grads[5]))
    far, *grads = lax.optimization_barrier((far, *grads))
    sums = {distance: add(grads[2 * distance], twin(grads[2 * distance + 1])) for distance in (3, 1, 0)}
    k, v = slice(0, ROWS), slice(ROWS, 2 * ROWS)
    key_left = left(sums[3][:, k])
    key_relay = add(sums[1][:, k], right(far[:, k]))
    value_relay = add(sums[3][:, v], left(far[:, v]))
    key_right, value_left = right(key_relay), left(value_relay)
    value_right = right(sums[1][:, v])
    key_sum = add(sums[0][:, k], key_right, key_left)
    value_sum = add(sums[0][:, v], value_right, value_left)
    sums = jnp.concatenate([key_sum, value_sum], axis=1)
    sums, ad_back = lax.optimization_barrier((sums, ad_back))
    return (*unpack(swap(ad_back)), *unpack(over_heads(sums), turned=True))


def solution(mesh):
    fine = Mesh(mesh.devices.reshape(mesh.devices.shape[0], XS, ZS, CS), ("batch", "x", "z", "core"))
    seq = ("x", "z", "core")
    rows = P("batch", seq, None)
    return jax.shard_map(
        local,
        mesh=fine,
        in_specs=(rows, rows, rows, rows, P("batch", seq)),
        out_specs=(rows, rows, rows, rows),
        check_vma=False,
    )
```

```python
import functools

import jax
import jax.numpy as jnp
from jax import lax
from jax.experimental import pallas as pl
from jax.experimental.pallas import tpu as pltpu
from jax.sharding import Mesh, PartitionSpec as P

HEADS = 8
HDIM = 128
ROWS = 128
TILE = 16
XS, ZS, CS = 4, 8, 2
CHUNKS = XS * ZS * CS
QB = 512
KB = 512
SLAB = 256
GROUP = 32
COLS = tuple(slice(i, i + SLAB) for i in range(0, QB, SLAB))
STEPS = CHUNKS * ROWS // KB
INV_ROOT = HDIM ** -0.5
LOG2E = 1.4426950408889634
NEG = -1e30

NT = (((1,), (1,)), ((), ()))
TN = (((0,), (0,)), ((), ()))


def dot(a, b, dims=(((1,), (0,)), ((), ()))):
    return lax.dot_general(a, b, dims, preferred_element_type=jnp.float32)


PIECES = ((0, 0, 8), (3, 0, 8), (1, 0, 8), (2, 0, 4), (2, 4, 4))
N_PIECES = 2 * len(PIECES)


def attention_kernel(at_ref, *refs):
    pieces, qd_in, ad_ref, grads, refs = (
        refs[:N_PIECES], refs[N_PIECES], refs[N_PIECES + 1], refs[N_PIECES + 2 : N_PIECES + 10], refs[N_PIECES + 10 :],
    )
    kvs_ref, qd_ref, s_scr, e_scr, dk_scr, dv_scr, acc_scr, dq_scr, don_scr, dont_scr, q_scr, qt_scr, ds_scr, now_scr, dp_scr, top_scr, tops_scr, delta_scr, sum_scr, qs_scr, sems, qsem = refs
    x, own_core = at_ref[0], at_ref[1]

    def first_chunk(distance, other):
        core = 1 - own_core if other else own_core
        return (lax.rem(x + distance, XS) * CS + core) * ZS

    copies = [pltpu.make_async_copy(qd_in, qd_ref, qsem.at[0])]
    for i, (distance, start, count) in enumerate(PIECES):
        for other in (0, 1):
            n = 2 * i + other
            copies.append(
                pltpu.make_async_copy(
                    pieces[n], kvs_ref.at[pl.ds(first_chunk(distance, other) + start, count)], sems.at[n]
                )
            )
    for copy in copies:
        copy.start()
    dk_scr[...] = jnp.zeros_like(dk_scr)
    dv_scr[...] = jnp.zeros_like(dv_scr)
    for copy in copies:
        copy.wait()

    key_scales = kvs_ref[:, 256:272, :].astype(jnp.float32)[:, 0, :]
    chunk = lax.broadcasted_iota(jnp.int32, key_scales.shape, 0)
    lane = lax.broadcasted_iota(jnp.int32, key_scales.shape, 1)
    core = (chunk // ZS) % CS
    parity = chunk % 2
    is_first = (core == 0) & (parity == 0) & (lane == 0)
    is_last = (core == 1) & (parity == 1) & (lane == ROWS - 1)

    def parts(step):
        base = (step // 4) * 16 + 2 * (step % 4)
        return (base, base + 8)

    def slab(step, half, start):
        return kvs_ref[pl.ds(parts(step)[half], 2), start : start + ROWS, :].reshape(SLAB, HDIM)

    def down(row):
        return jnp.broadcast_to(row, (ROWS, ROWS)).T

    def fold(tile, op):
        return op(tile.reshape(tile.shape[0] // 8, 8, tile.shape[1]), axis=0)

    def one_block(block, _):
        first = block * (QB // ROWS)

        def rows(start):
            return qd_ref[pl.ds(first, QB // ROWS), start : start + ROWS, :].reshape(QB, HDIM)

        own = qd_ref[pl.ds(first, QB // ROWS), 256:272, :].astype(jnp.float32)[:, 0, :]
        for i in range(QB // ROWS):
            qs_scr[:, i * ROWS : (i + 1) * ROWS] = jnp.broadcast_to(own[i : i + 1, :], (8, ROWS))
        low, high = jnp.min(own), jnp.max(own)
        n_steps = jnp.sum(jnp.where(is_first & (key_scales <= high), 1.0, 0.0)).astype(jnp.int32)
        n_steps = jnp.maximum(n_steps, 2)
        n_full = jnp.sum(jnp.where(is_last & (key_scales <= low), 1.0, 0.0)).astype(jnp.int32)

        def scores(masked, step):
            for half in range(KB // SLAB):
                k = slab(step, half, 0)
                if masked:
                    ks = [
                        down(kvs_ref[parts(step)[half] + i, 256:272, :].astype(jnp.float32)[0:1, :])
                        for i in range(SLAB // ROWS)
                    ]
                for cols in COLS:
                    s = dot(k, q_scr[cols, :], NT)
                    for r in range(0, SLAB, GROUP):
                        tile = s[r : r + GROUP, :]
                        if masked:
                            own_ks = ks[r // ROWS][r % ROWS : r % ROWS + GROUP, :]
                            tile = jnp.concatenate(
                                [
                                    jnp.where(
                                        own_ks <= qs_scr[0:1, cols.start + j : cols.start + j + ROWS],
                                        tile[:, j : j + ROWS],
                                        NEG,
                                    )
                                    for j in range(0, SLAB, ROWS)
                                ],
                                axis=1,
                            )
                        s_scr[half * SLAB + r : half * SLAB + r + GROUP, cols] = tile

        q_scr[...] = rows(0)
        qt_scr[...] = rows(0).astype(jnp.float32).T.astype(jnp.bfloat16)
        top_scr[...] = jnp.full_like(top_scr, NEG)
        sum_scr[...] = jnp.zeros_like(sum_scr)
        acc_scr[...] = jnp.zeros_like(acc_scr)

        def weigh(step):
            for half in range(KB // SLAB):
                own = slice(half * SLAB, (half + 1) * SLAB)
                acc_scr[...] += dot(slab(step, half, 128), now_scr[own, :], TN)

        def exponentials(step):
            top = fold(s_scr[0:GROUP, :], jnp.max)
            for r in range(GROUP, KB, GROUP):
                top = jnp.maximum(top, fold(s_scr[r : r + GROUP, :], jnp.max))
            top = jnp.ceil(jnp.max(top, axis=0, keepdims=True) * (INV_ROOT * LOG2E))
            top = jnp.maximum(top_scr[0:1, :], top)
            drop = jnp.exp2(top_scr[0:1, :] - top)
            top_scr[...] = jnp.broadcast_to(top, top_scr.shape)
            tops_scr[step] = jnp.broadcast_to(top, top_scr.shape)
            acc_scr[...] = acc_scr[...] * drop
            total = sum_scr[...] * drop
            for r in range(0, KB, GROUP):
                e = jnp.exp2(s_scr[r : r + GROUP, :] * (INV_ROOT * LOG2E) - top)
                total = total + fold(e, jnp.sum)
                e = e.astype(jnp.bfloat16)
                now_scr[r : r + GROUP, :] = e
                e_scr[step, r : r + GROUP, :] = e
            sum_scr[...] = total

        def forward(masked, step, _):
            weigh(step - 1)
            exponentials(step)
            scores(masked, step + 1)
            return 0

        scores(True, 0)
        exponentials(0)
        scores(True, 1)
        n_open = jnp.maximum(n_full - 1, 1)
        lax.fori_loop(1, n_open, functools.partial(forward, False), 0)
        lax.fori_loop(n_open, n_steps - 1, functools.partial(forward, True), 0)
        weigh(n_steps - 2)
        exponentials(n_steps - 1)
        weigh(n_steps - 1)
        inv = 1.0 / jnp.sum(sum_scr[...], axis=0, keepdims=True)
        attn = (acc_scr[...] * inv).T
        inv_rows = jnp.broadcast_to(inv, (HDIM, QB)).T
        for i in range(QB // ROWS):
            ad_ref[first + i, 0:128, :] = attn[i * ROWS : (i + 1) * ROWS, :].astype(jnp.bfloat16)
        do_n = (rows(128).astype(jnp.float32) * inv_rows).astype(jnp.bfloat16)
        don_scr[...] = do_n
        dont_scr[...] = do_n.astype(jnp.float32).T.astype(jnp.bfloat16)
        delta = jnp.sum(do_n.astype(jnp.float32) * attn, axis=1, keepdims=True)
        delta_scr[...] = jnp.broadcast_to(delta, (QB, HDIM)).T[0:8, :]
        dq_scr[...] = jnp.zeros_like(dq_scr)

        def dprobs(step):
            for half in range(KB // SLAB):
                v = slab(step, half, 128)
                for cols in COLS:
                    dp_scr[half * SLAB : (half + 1) * SLAB, cols] = dot(v, don_scr[cols, :], NT)

        def backward(step, _):
            drop = jnp.exp2(tops_scr[step, 0:1, :] - top_scr[0:1, :])
            delta = delta_scr[0:1, :]
            for r in range(0, KB, GROUP):
                e = e_scr[step, r : r + GROUP, :].astype(jnp.float32) * drop
                now_scr[r : r + GROUP, :] = e.astype(jnp.bfloat16)
                ds_scr[r : r + GROUP, :] = (e * (dp_scr[r : r + GROUP, :] - delta)).astype(jnp.bfloat16)
            for half in range(KB // SLAB):
                dv = dot(dont_scr[...], now_scr[half * SLAB : (half + 1) * SLAB, :], NT)
                for i in range(SLAB // ROWS):
                    dv_scr[parts(step)[half] + i] += dv[:, i * ROWS : (i + 1) * ROWS]
            dprobs(jnp.minimum(step + 1, STEPS - 1))
            for half in range(KB // SLAB):
                own = slice(half * SLAB, (half + 1) * SLAB)
                dk = dot(qt_scr[...], ds_scr[own, :], NT)
                for i in range(SLAB // ROWS):
                    dk_scr[parts(step)[half] + i] += dk[:, i * ROWS : (i + 1) * ROWS]
                dq_scr[...] += dot(slab(step, half, 0), ds_scr[own, :], TN)
            return 0

        dprobs(0)
        lax.fori_loop(0, n_steps, backward, 0)
        dq = (dq_scr[...] * INV_ROOT).T.astype(jnp.bfloat16)
        for i in range(QB // ROWS):
            ad_ref[first + i, 128:256, :] = dq[i * ROWS : (i + 1) * ROWS, :]
        return 0

    lax.fori_loop(0, ZS * ROWS // QB, one_block, 0)

    for distance in range(XS):
        for other in (0, 1):
            out = grads[2 * distance + other]
            base = first_chunk(distance, other)
            out[:, 0:128, :] = (dk_scr[pl.ds(base, ZS)] * INV_ROOT).astype(jnp.bfloat16)
            out[:, 128:256, :] = dv_scr[pl.ds(base, ZS)].astype(jnp.bfloat16)


def attention(at, pieces, qd):
    vmem = pl.BlockSpec(memory_space=pltpu.VMEM)
    outs = (jax.ShapeDtypeStruct((ZS, 2 * ROWS, HDIM), jnp.bfloat16),) * 9
    return pl.pallas_call(
        attention_kernel,
        out_shape=outs,
        in_specs=[pl.BlockSpec(memory_space=pltpu.SMEM)] + [vmem] * (N_PIECES + 1),
        out_specs=(vmem,) * len(outs),
        scratch_shapes=[
            pltpu.VMEM((CHUNKS, 2 * ROWS + TILE, HDIM), jnp.bfloat16),
            pltpu.VMEM((ZS, 2 * ROWS + TILE, HDIM), jnp.bfloat16),
            pltpu.VMEM((KB, QB), jnp.float32),
            pltpu.VMEM((STEPS, KB, QB), jnp.bfloat16),
            pltpu.VMEM((CHUNKS, ROWS, HDIM), jnp.float32),
            pltpu.VMEM((CHUNKS, ROWS, HDIM), jnp.float32),
            pltpu.VMEM((HDIM, QB), jnp.float32),
            pltpu.VMEM((HDIM, QB), jnp.float32),
            pltpu.VMEM((QB, HDIM), jnp.bfloat16),
            pltpu.VMEM((HDIM, QB), jnp.bfloat16),
            pltpu.VMEM((QB, HDIM), jnp.bfloat16),
            pltpu.VMEM((HDIM, QB), jnp.bfloat16),
            pltpu.VMEM((KB, QB), jnp.bfloat16),
            pltpu.VMEM((KB, QB), jnp.bfloat16),
            pltpu.VMEM((KB, QB), jnp.float32),
            pltpu.VMEM((8, QB), jnp.float32),
            pltpu.VMEM((STEPS, 8, QB), jnp.float32),
            pltpu.VMEM((8, QB), jnp.float32),
            pltpu.VMEM((8, QB), jnp.float32),
            pltpu.VMEM((8, QB), jnp.float32),
            pltpu.SemaphoreType.DMA((N_PIECES,)),
            pltpu.SemaphoreType.DMA((1,)),
        ],
        compiler_params=pltpu.CompilerParams(vmem_limit_bytes=34 * 1024 * 1024),
        cost_estimate=pl.CostEstimate(flops=8 * 10**9, bytes_accessed=10 * 2**20, transcendentals=5 * 10**6),
    )(at, *pieces, qd)


def pack_kernel(a_ref, b_ref, scale_ref, out_ref):
    scales = jnp.broadcast_to(scale_ref[...].astype(jnp.float32), (TILE, ROWS)).astype(jnp.bfloat16)
    for h in range(HEADS):
        out_ref[h, 0:128, :] = a_ref[0, :, h * HDIM : (h + 1) * HDIM]
        out_ref[h, 128:256, :] = b_ref[0, :, h * HDIM : (h + 1) * HDIM]
        out_ref[h, 256:272, :] = scales


def pack(a, b, scale_ids):
    vmem = pl.BlockSpec(memory_space=pltpu.VMEM)
    return pl.pallas_call(
        pack_kernel,
        out_shape=jax.ShapeDtypeStruct((HEADS, 2 * ROWS + TILE, HDIM), jnp.bfloat16),
        in_specs=[vmem] * 3,
        out_specs=vmem,
    )(a, b, scale_ids)


def unpack_kernel(in_ref, *outs, turned):
    for h in range(HEADS):
        for i, out in enumerate(outs):
            tile = in_ref[h, i * ROWS : (i + 1) * ROWS, :]
            if turned:
                tile = tile.astype(jnp.float32).T.astype(jnp.bfloat16)
            out[0, :, h * HDIM : (h + 1) * HDIM] = tile


def unpack(arr, turned=False):
    vmem = pl.BlockSpec(memory_space=pltpu.VMEM)
    rows = jax.ShapeDtypeStruct((1, ROWS, HEADS * HDIM), jnp.bfloat16)
    n = arr.shape[1] // ROWS
    kernel = functools.partial(unpack_kernel, turned=turned)
    return pl.pallas_call(kernel, out_shape=(rows,) * n, in_specs=[vmem], out_specs=(vmem,) * n)(arr)


def add(*arrs):
    total = arrs[0].astype(jnp.float32)
    for arr in arrs[1:]:
        total = total + arr.astype(jnp.float32)
    return total.astype(jnp.bfloat16)


def local(query, key, value, grad_attn, scale_ids):
    def over_heads(arr):
        return lax.all_to_all(arr, "z", split_axis=0, concat_axis=0, tiled=True)

    def right(arr):
        return lax.ppermute(arr, "x", [(i, (i + 1) % XS) for i in range(XS)])

    def left(arr):
        return lax.ppermute(arr, "x", [(i, (i + XS - 1) % XS) for i in range(XS)])

    def swap(arr):
        pairs = [
            (x * ZS + z, (XS - 1 - x if z >= ZS // 2 else x) * ZS + z) for x in range(XS) for z in range(ZS)
        ]
        return lax.ppermute(arr, ("x", "z"), pairs)

    def twin(arr):
        return lax.ppermute(arr, "core", [(0, 1), (1, 0)])

    half = ZS // 2
    at = jnp.stack([lax.axis_index("x"), lax.axis_index("core")]).astype(jnp.int32)

    kvs = over_heads(pack(key, value, scale_ids))
    swapped = swap(pack(query, grad_attn, scale_ids))
    kvs, swapped = lax.optimization_barrier((kvs, swapped))
    from_left, from_right = right(kvs), left(kvs)
    qd = over_heads(swapped)
    opposite_a, opposite_b = right(from_left[:half]), left(from_right[half:])
    pieces = []
    for piece in (kvs, from_left, from_right, opposite_a, opposite_b):
        pieces += [piece, twin(piece)]

    ad, *grads = attention(at, pieces, qd)

    far = add(grads[4], twin(grads[5]))
    far, *grads = lax.optimization_barrier((far, *grads))
    sums = {distance: add(grads[2 * distance], twin(grads[2 * distance + 1])) for distance in (3, 1, 0)}
    ad, sums[1], sums[3] = lax.optimization_barrier((ad, sums[1], sums[3]))
    ad_back = over_heads(ad)
    k, v = slice(0, ROWS), slice(ROWS, 2 * ROWS)
    key_left = left(sums[3][:, k])
    key_relay = add(sums[1][:, k], right(far[:, k]))
    value_relay = add(sums[3][:, v], left(far[:, v]))
    key_right, value_left = right(key_relay), left(value_relay)
    value_right = right(sums[1][:, v])
    key_right, ad_back = lax.optimization_barrier((key_right, ad_back))
    key_sum = add(sums[0][:, k], key_right, key_left)
    value_sum = add(sums[0][:, v], value_right, value_left)
    sums = jnp.concatenate([key_sum, value_sum], axis=1)
    return (*unpack(swap(ad_back)), *unpack(over_heads(sums), turned=True))


def solution(mesh):
    fine = Mesh(mesh.devices.reshape(mesh.devices.shape[0], XS, ZS, CS), ("batch", "x", "z", "core"))
    seq = ("x", "z", "core")
    rows = P("batch", seq, None)
    return jax.shard_map(
        local,
        mesh=fine,
        in_specs=(rows, rows, rows, rows, P("batch", seq)),
        out_specs=(rows, rows, rows, rows),
        check_vma=False,
    )
```

```python
import functools

import jax
import jax.numpy as jnp
from jax import lax
from jax.experimental import pallas as pl
from jax.experimental.pallas import tpu as pltpu
from jax.sharding import Mesh, PartitionSpec as P

HEADS = 8
HDIM = 128
ROWS = 128
TILE = 16
XS, ZS, CS = 4, 8, 2
CHUNKS = XS * ZS * CS
QB = 512
KB = 512
SLAB = 256
GROUP = 32
ALL, LATE = slice(0, QB), slice(QB // 2, QB)
STEPS = CHUNKS * ROWS // KB
INV_ROOT = HDIM ** -0.5
LOG2E = 1.4426950408889634
NEG = -1e30

NT = (((1,), (1,)), ((), ()))
TN = (((0,), (0,)), ((), ()))


def dot(a, b, dims=(((1,), (0,)), ((), ()))):
    return lax.dot_general(a, b, dims, preferred_element_type=jnp.float32)


PIECES = ((0, 0, 8), (3, 0, 8), (1, 0, 8), (2, 0, 4), (2, 4, 4))
N_PIECES = 2 * len(PIECES)


def columns(wide):
    return [slice(i, i + SLAB) for i in range(wide.start, wide.stop, SLAB)]


def attention_kernel(at_ref, *refs):
    pieces, qd_in, ad_ref, grads, refs = (
        refs[:N_PIECES], refs[N_PIECES], refs[N_PIECES + 1], refs[N_PIECES + 2 : N_PIECES + 10], refs[N_PIECES + 10 :],
    )
    kvs_ref, qd_ref, s_scr, e_scr, dk_scr, dv_scr, acc_scr, dq_scr, don_scr, dont_scr, q_scr, qt_scr, ds_scr, now_scr, dp_scr, top_scr, tops_scr, delta_scr, sum_scr, qs_scr, sems, qsem = refs
    x, own_core = at_ref[0], at_ref[1]

    def first_chunk(distance, other):
        core = 1 - own_core if other else own_core
        return (lax.rem(x + distance, XS) * CS + core) * ZS

    copies = [pltpu.make_async_copy(qd_in, qd_ref, qsem.at[0])]
    for i, (distance, start, count) in enumerate(PIECES):
        for other in (0, 1):
            n = 2 * i + other
            copies.append(
                pltpu.make_async_copy(
                    pieces[n], kvs_ref.at[pl.ds(first_chunk(distance, other) + start, count)], sems.at[n]
                )
            )
    for copy in copies:
        copy.start()
    dk_scr[...] = jnp.zeros_like(dk_scr)
    dv_scr[...] = jnp.zeros_like(dv_scr)
    for copy in copies:
        copy.wait()

    key_scales = kvs_ref[:, 256:272, :].astype(jnp.float32)[:, 0, :]
    chunk = lax.broadcasted_iota(jnp.int32, key_scales.shape, 0)
    lane = lax.broadcasted_iota(jnp.int32, key_scales.shape, 1)
    core = (chunk // ZS) % CS
    parity = chunk % 2
    is_first = (core == 0) & (parity == 0) & (lane == 0)
    is_last = (core == 1) & (parity == 1) & (lane == ROWS - 1)

    def parts(step):
        base = (step // 4) * 16 + 2 * (step % 4)
        return (base, base + 8)

    def slab(step, half, start):
        return kvs_ref[pl.ds(parts(step)[half], 2), start : start + ROWS, :].reshape(SLAB, HDIM)

    def down(row):
        return jnp.broadcast_to(row, (ROWS, ROWS)).T

    def fold(tile, op):
        return op(tile.reshape(tile.shape[0] // 8, 8, tile.shape[1]), axis=0)

    def one_block(block, _):
        first = block * (QB // ROWS)

        def rows(start):
            return qd_ref[pl.ds(first, QB // ROWS), start : start + ROWS, :].reshape(QB, HDIM)

        own = qd_ref[pl.ds(first, QB // ROWS), 256:272, :].astype(jnp.float32)[:, 0, :]
        for i in range(QB // ROWS):
            qs_scr[:, i * ROWS : (i + 1) * ROWS] = jnp.broadcast_to(own[i : i + 1, :], (8, ROWS))
        late = own[QB // ROWS // 2 :, :]

        def needed(rows):
            return jnp.sum(jnp.where(is_first & (key_scales <= jnp.max(rows)), 1.0, 0.0)).astype(jnp.int32)

        def open_to(rows):
            return jnp.sum(jnp.where(is_last & (key_scales <= jnp.min(rows)), 1.0, 0.0)).astype(jnp.int32)

        n_wide = jnp.maximum(needed(own[: QB // ROWS // 2, :]), 2)
        n_steps = jnp.maximum(needed(late), n_wide)
        n_wide = jnp.where(n_steps - n_wide == 1, n_steps, n_wide)

        def scores(wide, masked, step):
            for half in range(KB // SLAB):
                k = slab(step, half, 0)
                if masked:
                    ks = [
                        down(kvs_ref[parts(step)[half] + i, 256:272, :].astype(jnp.float32)[0:1, :])
                        for i in range(SLAB // ROWS)
                    ]
                for cols in columns(wide):
                    s = dot(k, q_scr[cols, :], NT)
                    for r in range(0, SLAB, GROUP):
                        tile = s[r : r + GROUP, :]
                        if masked:
                            own_ks = ks[r // ROWS][r % ROWS : r % ROWS + GROUP, :]
                            tile = jnp.concatenate(
                                [
                                    jnp.where(
                                        own_ks <= qs_scr[0:1, cols.start + j : cols.start + j + ROWS],
                                        tile[:, j : j + ROWS],
                                        NEG,
                                    )
                                    for j in range(0, SLAB, ROWS)
                                ],
                                axis=1,
                            )
                        s_scr[half * SLAB + r : half * SLAB + r + GROUP, cols] = tile

        q_scr[...] = rows(0)
        qt_scr[...] = rows(0).astype(jnp.float32).T.astype(jnp.bfloat16)
        top_scr[...] = jnp.full_like(top_scr, NEG)
        sum_scr[...] = jnp.zeros_like(sum_scr)
        acc_scr[...] = jnp.zeros_like(acc_scr)

        def weigh(wide, step):
            for half in range(KB // SLAB):
                own = slice(half * SLAB, (half + 1) * SLAB)
                acc_scr[:, wide] += dot(slab(step, half, 128), now_scr[own, wide], TN)

        def exponentials(wide, step):
            top = fold(s_scr[0:GROUP, wide], jnp.max)
            for r in range(GROUP, KB, GROUP):
                top = jnp.maximum(top, fold(s_scr[r : r + GROUP, wide], jnp.max))
            top = jnp.ceil(jnp.max(top, axis=0, keepdims=True) * (INV_ROOT * LOG2E))
            top = jnp.maximum(top_scr[0:1, wide], top)
            drop = jnp.exp2(top_scr[0:1, wide] - top)
            top_scr[:, wide] = jnp.broadcast_to(top, (8, top.shape[1]))
            tops_scr[step, :, wide] = jnp.broadcast_to(top, (8, top.shape[1]))
            acc_scr[:, wide] = acc_scr[:, wide] * drop
            total = sum_scr[:, wide] * drop
            for r in range(0, KB, GROUP):
                e = jnp.exp2(s_scr[r : r + GROUP, wide] * (INV_ROOT * LOG2E) - top)
                total = total + fold(e, jnp.sum)
                e = e.astype(jnp.bfloat16)
                now_scr[r : r + GROUP, wide] = e
                e_scr[step, r : r + GROUP, wide] = e
            sum_scr[:, wide] = total

        def forward(wide, masked, step, _):
            weigh(wide, step - 1)
            exponentials(wide, step)
            scores(wide, masked, step + 1)
            return 0

        def forward_pass(wide, start, n_open, end):
            scores(wide, True, start)
            exponentials(wide, start)
            scores(wide, True, start + 1)
            n_open = jnp.minimum(jnp.maximum(n_open - 1, start + 1), end - 1)
            lax.fori_loop(start + 1, n_open, functools.partial(forward, wide, False), 0)
            lax.fori_loop(n_open, end - 1, functools.partial(forward, wide, True), 0)
            weigh(wide, end - 2)
            exponentials(wide, end - 1)
            weigh(wide, end - 1)

        forward_pass(ALL, 0, open_to(own), n_wide)

        @pl.when(n_steps > n_wide)
        def _():
            forward_pass(LATE, n_wide, open_to(late), n_steps)

        inv = 1.0 / jnp.sum(sum_scr[...], axis=0, keepdims=True)
        attn = (acc_scr[...] * inv).T
        inv_rows = jnp.broadcast_to(inv, (HDIM, QB)).T
        for i in range(QB // ROWS):
            ad_ref[first + i, 0:128, :] = attn[i * ROWS : (i + 1) * ROWS, :].astype(jnp.bfloat16)
        do_n = (rows(128).astype(jnp.float32) * inv_rows).astype(jnp.bfloat16)
        don_scr[...] = do_n
        dont_scr[...] = do_n.astype(jnp.float32).T.astype(jnp.bfloat16)
        delta = jnp.sum(do_n.astype(jnp.float32) * attn, axis=1, keepdims=True)
        delta_scr[...] = jnp.broadcast_to(delta, (QB, HDIM)).T[0:8, :]
        dq_scr[...] = jnp.zeros_like(dq_scr)

        def dprobs(wide, step):
            for half in range(KB // SLAB):
                v = slab(step, half, 128)
                for cols in columns(wide):
                    dp_scr[half * SLAB : (half + 1) * SLAB, cols] = dot(v, don_scr[cols, :], NT)

        def backward(wide, step, _):
            drop = jnp.exp2(tops_scr[step, 0:1, wide] - top_scr[0:1, wide])
            delta = delta_scr[0:1, wide]
            for r in range(0, KB, GROUP):
                e = e_scr[step, r : r + GROUP, wide].astype(jnp.float32) * drop
                now_scr[r : r + GROUP, wide] = e.astype(jnp.bfloat16)
                ds_scr[r : r + GROUP, wide] = (e * (dp_scr[r : r + GROUP, wide] - delta)).astype(jnp.bfloat16)
            for half in range(KB // SLAB):
                dv = dot(dont_scr[:, wide], now_scr[half * SLAB : (half + 1) * SLAB, wide], NT)
                for i in range(SLAB // ROWS):
                    dv_scr[parts(step)[half] + i] += dv[:, i * ROWS : (i + 1) * ROWS]
            dprobs(wide, jnp.minimum(step + 1, STEPS - 1))
            for half in range(KB // SLAB):
                own = slice(half * SLAB, (half + 1) * SLAB)
                dk = dot(qt_scr[:, wide], ds_scr[own, wide], NT)
                for i in range(SLAB // ROWS):
                    dk_scr[parts(step)[half] + i] += dk[:, i * ROWS : (i + 1) * ROWS]
                dq_scr[:, wide] += dot(slab(step, half, 0), ds_scr[own, wide], TN)
            return 0

        def backward_pass(wide, start, end):
            dprobs(wide, start)
            lax.fori_loop(start, end, functools.partial(backward, wide), 0)

        backward_pass(ALL, 0, n_wide)

        @pl.when(n_steps > n_wide)
        def _():
            backward_pass(LATE, n_wide, n_steps)

        dq = (dq_scr[...] * INV_ROOT).T.astype(jnp.bfloat16)
        for i in range(QB // ROWS):
            ad_ref[first + i, 128:256, :] = dq[i * ROWS : (i + 1) * ROWS, :]
        return 0

    lax.fori_loop(0, ZS * ROWS // QB, one_block, 0)

    for distance in range(XS):
        for other in (0, 1):
            out = grads[2 * distance + other]
            base = first_chunk(distance, other)
            out[:, 0:128, :] = (dk_scr[pl.ds(base, ZS)] * INV_ROOT).astype(jnp.bfloat16)
            out[:, 128:256, :] = dv_scr[pl.ds(base, ZS)].astype(jnp.bfloat16)


def attention(at, pieces, qd):
    vmem = pl.BlockSpec(memory_space=pltpu.VMEM)
    outs = (jax.ShapeDtypeStruct((ZS, 2 * ROWS, HDIM), jnp.bfloat16),) * 9
    return pl.pallas_call(
        attention_kernel,
        out_shape=outs,
        in_specs=[pl.BlockSpec(memory_space=pltpu.SMEM)] + [vmem] * (N_PIECES + 1),
        out_specs=(vmem,) * len(outs),
        scratch_shapes=[
            pltpu.VMEM((CHUNKS, 2 * ROWS + TILE, HDIM), jnp.bfloat16),
            pltpu.VMEM((ZS, 2 * ROWS + TILE, HDIM), jnp.bfloat16),
            pltpu.VMEM((KB, QB), jnp.float32),
            pltpu.VMEM((STEPS, KB, QB), jnp.bfloat16),
            pltpu.VMEM((CHUNKS, ROWS, HDIM), jnp.float32),
            pltpu.VMEM((CHUNKS, ROWS, HDIM), jnp.float32),
            pltpu.VMEM((HDIM, QB), jnp.float32),
            pltpu.VMEM((HDIM, QB), jnp.float32),
            pltpu.VMEM((QB, HDIM), jnp.bfloat16),
            pltpu.VMEM((HDIM, QB), jnp.bfloat16),
            pltpu.VMEM((QB, HDIM), jnp.bfloat16),
            pltpu.VMEM((HDIM, QB), jnp.bfloat16),
            pltpu.VMEM((KB, QB), jnp.bfloat16),
            pltpu.VMEM((KB, QB), jnp.bfloat16),
            pltpu.VMEM((KB, QB), jnp.float32),
            pltpu.VMEM((8, QB), jnp.float32),
            pltpu.VMEM((STEPS, 8, QB), jnp.float32),
            pltpu.VMEM((8, QB), jnp.float32),
            pltpu.VMEM((8, QB), jnp.float32),
            pltpu.VMEM((8, QB), jnp.float32),
            pltpu.SemaphoreType.DMA((N_PIECES,)),
            pltpu.SemaphoreType.DMA((1,)),
        ],
        compiler_params=pltpu.CompilerParams(vmem_limit_bytes=34 * 1024 * 1024),
        cost_estimate=pl.CostEstimate(flops=8 * 10**9, bytes_accessed=10 * 2**20, transcendentals=5 * 10**6),
    )(at, *pieces, qd)


def pack_kernel(a_ref, b_ref, scale_ref, out_ref):
    scales = jnp.broadcast_to(scale_ref[...].astype(jnp.float32), (TILE, ROWS)).astype(jnp.bfloat16)
    for h in range(HEADS):
        out_ref[h, 0:128, :] = a_ref[0, :, h * HDIM : (h + 1) * HDIM]
        out_ref[h, 128:256, :] = b_ref[0, :, h * HDIM : (h + 1) * HDIM]
        out_ref[h, 256:272, :] = scales


def pack(a, b, scale_ids):
    vmem = pl.BlockSpec(memory_space=pltpu.VMEM)
    return pl.pallas_call(
        pack_kernel,
        out_shape=jax.ShapeDtypeStruct((HEADS, 2 * ROWS + TILE, HDIM), jnp.bfloat16),
        in_specs=[vmem] * 3,
        out_specs=vmem,
    )(a, b, scale_ids)


def unpack_kernel(ad_ref, dkv_ref, attn_ref, dq_ref, dk_ref, dv_ref, buf, sems):
    copies = [pltpu.make_async_copy(ref, buf.at[i], sems.at[i]) for i, ref in enumerate((ad_ref, dkv_ref))]
    for copy in copies:
        copy.start()
    for which, outs in enumerate(((attn_ref, dq_ref), (dk_ref, dv_ref))):
        copies[which].wait()
        for h in range(HEADS):
            for i, out in enumerate(outs):
                tile = buf[which, h, i * ROWS : (i + 1) * ROWS, :]
                if which:
                    tile = tile.astype(jnp.float32).T.astype(jnp.bfloat16)
                out[0, :, h * HDIM : (h + 1) * HDIM] = tile


def unpack(ad, dkv):
    vmem = pl.BlockSpec(memory_space=pltpu.VMEM)
    rows = jax.ShapeDtypeStruct((1, ROWS, HEADS * HDIM), jnp.bfloat16)
    return pl.pallas_call(
        unpack_kernel,
        out_shape=(rows,) * 4,
        in_specs=[pl.BlockSpec(memory_space=pl.ANY)] * 2,
        out_specs=(vmem,) * 4,
        scratch_shapes=[
            pltpu.VMEM((2, HEADS, 2 * ROWS, HDIM), jnp.bfloat16),
            pltpu.SemaphoreType.DMA((2,)),
        ],
    )(ad, dkv)


def add(*arrs):
    total = arrs[0].astype(jnp.float32)
    for arr in arrs[1:]:
        total = total + arr.astype(jnp.float32)
    return total.astype(jnp.bfloat16)


def local(query, key, value, grad_attn, scale_ids):
    def over_heads(arr):
        return lax.all_to_all(arr, "z", split_axis=0, concat_axis=0, tiled=True)

    def right(arr):
        return lax.ppermute(arr, "x", [(i, (i + 1) % XS) for i in range(XS)])

    def left(arr):
        return lax.ppermute(arr, "x", [(i, (i + XS - 1) % XS) for i in range(XS)])

    def swap(arr):
        pairs = [
            (x * ZS + z, (XS - 1 - x if z >= ZS // 2 else x) * ZS + z) for x in range(XS) for z in range(ZS)
        ]
        return lax.ppermute(arr, ("x", "z"), pairs)

    def twin(arr):
        return lax.ppermute(arr, "core", [(0, 1), (1, 0)])

    half = ZS // 2
    at = jnp.stack([lax.axis_index("x"), lax.axis_index("core")]).astype(jnp.int32)

    kvs = over_heads(pack(key, value, scale_ids))
    swapped = swap(pack(query, grad_attn, scale_ids))
    kvs, swapped = lax.optimization_barrier((kvs, swapped))
    from_left, from_right = right(kvs), left(kvs)
    qd = over_heads(swapped)
    opposite_a, opposite_b = right(from_left[:half]), left(from_right[half:])
    pieces = []
    for piece in (kvs, from_left, from_right, opposite_a, opposite_b):
        pieces += [piece, twin(piece)]

    ad, *grads = attention(at, pieces, qd)

    far = add(grads[4], twin(grads[5]))
    far, *grads = lax.optimization_barrier((far, *grads))
    sums = {distance: add(grads[2 * distance], twin(grads[2 * distance + 1])) for distance in (3, 1, 0)}
    ad, sums[1], sums[3] = lax.optimization_barrier((ad, sums[1], sums[3]))
    ad_back = over_heads(ad)
    k, v = slice(0, ROWS), slice(ROWS, 2 * ROWS)
    key_left = left(sums[3][:, k])
    key_relay = add(sums[1][:, k], right(far[:, k]))
    value_relay = add(sums[3][:, v], left(far[:, v]))
    key_right, value_left = right(key_relay), left(value_relay)
    value_right = right(sums[1][:, v])
    key_right, ad_back = lax.optimization_barrier((key_right, ad_back))
    key_sum = add(sums[0][:, k], key_right, key_left)
    value_sum = add(sums[0][:, v], value_right, value_left)
    sums = jnp.concatenate([key_sum, value_sum], axis=1)
    return unpack(swap(ad_back), over_heads(sums))


def solution(mesh):
    fine = Mesh(mesh.devices.reshape(mesh.devices.shape[0], XS, ZS, CS), ("batch", "x", "z", "core"))
    seq = ("x", "z", "core")
    rows = P("batch", seq, None)
    return jax.shard_map(
        local,
        mesh=fine,
        in_specs=(rows, rows, rows, rows, P("batch", seq)),
        out_specs=(rows, rows, rows, rows),
        check_vma=False,
    )
```

```python
import functools

import jax
import jax.numpy as jnp
from jax import lax
from jax.experimental import pallas as pl
from jax.experimental.pallas import tpu as pltpu
from jax.sharding import Mesh, PartitionSpec as P

HEADS = 8
HDIM = 128
ROWS = 128
TILE = 16
XS, ZS, CS = 4, 8, 2
CHUNKS = XS * ZS * CS
QB = 512
KB = 512
SLAB = 256
GROUP = 32
ALL, LATE = slice(0, QB), slice(QB // 2, QB)
STEPS = CHUNKS * ROWS // KB
INV_ROOT = HDIM ** -0.5
LOG2E = 1.4426950408889634
NEG = -1e30

NT = (((1,), (1,)), ((), ()))
TN = (((0,), (0,)), ((), ()))


def dot(a, b, dims=(((1,), (0,)), ((), ()))):
    return lax.dot_general(a, b, dims, preferred_element_type=jnp.float32)


PIECES = ((0, 0, 8), (3, 0, 8), (1, 0, 8), (2, 0, 4), (2, 4, 4))
N_PIECES = 2 * len(PIECES)


def columns(wide):
    return [slice(i, i + SLAB) for i in range(wide.start, wide.stop, SLAB)]


def attention_kernel(at_ref, *refs):
    pieces, qd_in, ad_ref, grads, refs = (
        refs[:N_PIECES], refs[N_PIECES], refs[N_PIECES + 1], refs[N_PIECES + 2 : N_PIECES + 10], refs[N_PIECES + 10 :],
    )
    kvs_ref, qd_ref, s_scr, e_scr, dk_scr, dv_scr, acc_scr, dq_scr, don_scr, dont_scr, q_scr, qt_scr, ds_scr, now_scr, dp_scr, top_scr, tops_scr, delta_scr, sum_scr, qs_scr, sems, qsem = refs
    x, own_core = at_ref[0], at_ref[1]

    def first_chunk(distance, other):
        core = 1 - own_core if other else own_core
        return (lax.rem(x + distance, XS) * CS + core) * ZS

    copies = [pltpu.make_async_copy(qd_in, qd_ref, qsem.at[0])]
    for i, (distance, start, count) in enumerate(PIECES):
        for other in (0, 1):
            n = 2 * i + other
            copies.append(
                pltpu.make_async_copy(
                    pieces[n], kvs_ref.at[pl.ds(first_chunk(distance, other) + start, count)], sems.at[n]
                )
            )
    for copy in copies:
        copy.start()
    dk_scr[...] = jnp.zeros_like(dk_scr)
    dv_scr[...] = jnp.zeros_like(dv_scr)
    for copy in copies:
        copy.wait()

    key_scales = kvs_ref[:, 256:272, :].astype(jnp.float32)[:, 0, :]
    chunk = lax.broadcasted_iota(jnp.int32, key_scales.shape, 0)
    lane = lax.broadcasted_iota(jnp.int32, key_scales.shape, 1)
    core = (chunk // ZS) % CS
    parity = chunk % 2
    is_first = (core == 0) & (parity == 0) & (lane == 0)
    is_last = (core == 1) & (parity == 1) & (lane == ROWS - 1)

    def parts(step):
        base = (step // 4) * 16 + 2 * (step % 4)
        return (base, base + 8)

    def slab(step, half, start):
        return kvs_ref[pl.ds(parts(step)[half], 2), start : start + ROWS, :].reshape(SLAB, HDIM)

    def down(row):
        return jnp.broadcast_to(row, (ROWS, ROWS)).T

    def fold(tile, op):
        return op(tile.reshape(tile.shape[0] // 8, 8, tile.shape[1]), axis=0)

    def one_block(block, _):
        first = block * (QB // ROWS)

        def rows(start):
            return qd_ref[pl.ds(first, QB // ROWS), start : start + ROWS, :].reshape(QB, HDIM)

        own = qd_ref[pl.ds(first, QB // ROWS), 256:272, :].astype(jnp.float32)[:, 0, :]
        for i in range(QB // ROWS):
            qs_scr[:, i * ROWS : (i + 1) * ROWS] = jnp.broadcast_to(own[i : i + 1, :], (8, ROWS))
        late = own[QB // ROWS // 2 :, :]

        def needed(rows):
            return jnp.sum(jnp.where(is_first & (key_scales <= jnp.max(rows)), 1.0, 0.0)).astype(jnp.int32)

        def open_to(rows):
            return jnp.sum(jnp.where(is_last & (key_scales <= jnp.min(rows)), 1.0, 0.0)).astype(jnp.int32)

        n_wide = jnp.maximum(needed(own[: QB // ROWS // 2, :]), 2)
        n_steps = jnp.maximum(needed(late), n_wide)
        n_wide = jnp.where(n_steps - n_wide == 1, n_steps, n_wide)

        def scores(wide, masked, step):
            for half in range(KB // SLAB):
                k = slab(step, half, 0)
                if masked:
                    ks = [
                        down(kvs_ref[parts(step)[half] + i, 256:272, :].astype(jnp.float32)[0:1, :])
                        for i in range(SLAB // ROWS)
                    ]
                for cols in columns(wide):
                    s = dot(k, q_scr[cols, :], NT)
                    for r in range(0, SLAB, GROUP):
                        tile = s[r : r + GROUP, :]
                        if masked:
                            own_ks = ks[r // ROWS][r % ROWS : r % ROWS + GROUP, :]
                            tile = jnp.concatenate(
                                [
                                    jnp.where(
                                        own_ks <= qs_scr[0:1, cols.start + j : cols.start + j + ROWS],
                                        tile[:, j : j + ROWS],
                                        NEG,
                                    )
                                    for j in range(0, SLAB, ROWS)
                                ],
                                axis=1,
                            )
                        s_scr[half * SLAB + r : half * SLAB + r + GROUP, cols] = tile

        q_scr[...] = rows(0)
        qt_scr[...] = rows(0).astype(jnp.float32).T.astype(jnp.bfloat16)
        top_scr[...] = jnp.full_like(top_scr, NEG)
        sum_scr[...] = jnp.zeros_like(sum_scr)
        acc_scr[...] = jnp.zeros_like(acc_scr)

        def weigh(wide, step):
            for half in range(KB // SLAB):
                own = slice(half * SLAB, (half + 1) * SLAB)
                acc_scr[:, wide] += dot(slab(step, half, 128), now_scr[own, wide], TN)

        def exponentials(wide, step):
            top = fold(s_scr[0:GROUP, wide], jnp.max)
            for r in range(GROUP, KB, GROUP):
                top = jnp.maximum(top, fold(s_scr[r : r + GROUP, wide], jnp.max))
            top = jnp.ceil(jnp.max(top, axis=0, keepdims=True) * (INV_ROOT * LOG2E))
            top = jnp.maximum(top_scr[0:1, wide], top)
            drop = jnp.exp2(top_scr[0:1, wide] - top)
            top_scr[:, wide] = jnp.broadcast_to(top, (8, top.shape[1]))
            tops_scr[step, :, wide] = jnp.broadcast_to(top, (8, top.shape[1]))
            acc_scr[:, wide] = acc_scr[:, wide] * drop
            total = sum_scr[:, wide] * drop
            for r in range(0, KB, GROUP):
                e = jnp.exp2(s_scr[r : r + GROUP, wide] * (INV_ROOT * LOG2E) - top)
                total = total + fold(e, jnp.sum)
                e = e.astype(jnp.bfloat16)
                now_scr[r : r + GROUP, wide] = e
                e_scr[step, r : r + GROUP, wide] = e
            sum_scr[:, wide] = total

        def forward(wide, masked, step, _):
            weigh(wide, step - 1)
            exponentials(wide, step)
            scores(wide, masked, step + 1)
            return 0

        def forward_pass(wide, start, n_open, end):
            scores(wide, True, start)
            exponentials(wide, start)
            scores(wide, True, start + 1)
            n_open = jnp.minimum(jnp.maximum(n_open - 1, start + 1), end - 1)
            lax.fori_loop(start + 1, n_open, functools.partial(forward, wide, False), 0)
            lax.fori_loop(n_open, end - 1, functools.partial(forward, wide, True), 0)
            weigh(wide, end - 2)
            exponentials(wide, end - 1)
            weigh(wide, end - 1)

        forward_pass(ALL, 0, open_to(own), n_wide)

        @pl.when(n_steps > n_wide)
        def _():
            forward_pass(LATE, n_wide, open_to(late), n_steps)

        inv = 1.0 / jnp.sum(sum_scr[...], axis=0, keepdims=True)
        attn = (acc_scr[...] * inv).T
        inv_rows = jnp.broadcast_to(inv, (HDIM, QB)).T
        for i in range(QB // ROWS):
            ad_ref[first + i, 0:128, :] = attn[i * ROWS : (i + 1) * ROWS, :].astype(jnp.bfloat16)
        do_n = (rows(128).astype(jnp.float32) * inv_rows).astype(jnp.bfloat16)
        don_scr[...] = do_n
        dont_scr[...] = do_n.astype(jnp.float32).T.astype(jnp.bfloat16)
        delta = jnp.sum(do_n.astype(jnp.float32) * attn, axis=1, keepdims=True)
        delta_scr[...] = jnp.broadcast_to(delta, (QB, HDIM)).T[0:8, :]
        dq_scr[...] = jnp.zeros_like(dq_scr)

        def dprobs(wide, step):
            for half in range(KB // SLAB):
                v = slab(step, half, 128)
                for cols in columns(wide):
                    dp_scr[half * SLAB : (half + 1) * SLAB, cols] = dot(v, don_scr[cols, :], NT)

        def backward(wide, step, _):
            drop = jnp.exp2(tops_scr[step, 0:1, wide] - top_scr[0:1, wide])
            delta = delta_scr[0:1, wide]
            for r in range(0, KB, GROUP):
                e = e_scr[step, r : r + GROUP, wide].astype(jnp.float32) * drop
                now_scr[r : r + GROUP, wide] = e.astype(jnp.bfloat16)
                ds_scr[r : r + GROUP, wide] = (e * (dp_scr[r : r + GROUP, wide] - delta)).astype(jnp.bfloat16)
            for half in range(KB // SLAB):
                dv = dot(dont_scr[:, wide], now_scr[half * SLAB : (half + 1) * SLAB, wide], NT)
                for i in range(SLAB // ROWS):
                    dv_scr[parts(step)[half] + i] += dv[:, i * ROWS : (i + 1) * ROWS]
            dprobs(wide, jnp.minimum(step + 1, STEPS - 1))
            for half in range(KB // SLAB):
                own = slice(half * SLAB, (half + 1) * SLAB)
                dk = dot(qt_scr[:, wide], ds_scr[own, wide], NT)
                for i in range(SLAB // ROWS):
                    dk_scr[parts(step)[half] + i] += dk[:, i * ROWS : (i + 1) * ROWS]
                dq_scr[:, wide] += dot(slab(step, half, 0), ds_scr[own, wide], TN)
            return 0

        def backward_pass(wide, start, end):
            dprobs(wide, start)
            lax.fori_loop(start, end, functools.partial(backward, wide), 0)

        backward_pass(ALL, 0, n_wide)

        @pl.when(n_steps > n_wide)
        def _():
            backward_pass(LATE, n_wide, n_steps)

        dq = (dq_scr[...] * INV_ROOT).T.astype(jnp.bfloat16)
        for i in range(QB // ROWS):
            ad_ref[first + i, 128:256, :] = dq[i * ROWS : (i + 1) * ROWS, :]
        return 0

    lax.fori_loop(0, ZS * ROWS // QB, one_block, 0)

    for distance in range(XS):
        for other in (0, 1):
            out = grads[2 * distance + other]
            base = first_chunk(distance, other)
            out[:, 0:128, :] = (dk_scr[pl.ds(base, ZS)] * INV_ROOT).astype(jnp.bfloat16)
            out[:, 128:256, :] = dv_scr[pl.ds(base, ZS)].astype(jnp.bfloat16)


def attention(at, pieces, qd):
    vmem = pl.BlockSpec(memory_space=pltpu.VMEM)
    outs = (jax.ShapeDtypeStruct((ZS, 2 * ROWS, HDIM), jnp.bfloat16),) * 9
    return pl.pallas_call(
        attention_kernel,
        out_shape=outs,
        in_specs=[pl.BlockSpec(memory_space=pltpu.SMEM)] + [vmem] * (N_PIECES + 1),
        out_specs=(vmem,) * len(outs),
        scratch_shapes=[
            pltpu.VMEM((CHUNKS, 2 * ROWS + TILE, HDIM), jnp.bfloat16),
            pltpu.VMEM((ZS, 2 * ROWS + TILE, HDIM), jnp.bfloat16),
            pltpu.VMEM((KB, QB), jnp.float32),
            pltpu.VMEM((STEPS, KB, QB), jnp.bfloat16),
            pltpu.VMEM((CHUNKS, ROWS, HDIM), jnp.float32),
            pltpu.VMEM((CHUNKS, ROWS, HDIM), jnp.float32),
            pltpu.VMEM((HDIM, QB), jnp.float32),
            pltpu.VMEM((HDIM, QB), jnp.float32),
            pltpu.VMEM((QB, HDIM), jnp.bfloat16),
            pltpu.VMEM((HDIM, QB), jnp.bfloat16),
            pltpu.VMEM((QB, HDIM), jnp.bfloat16),
            pltpu.VMEM((HDIM, QB), jnp.bfloat16),
            pltpu.VMEM((KB, QB), jnp.bfloat16),
            pltpu.VMEM((KB, QB), jnp.bfloat16),
            pltpu.VMEM((KB, QB), jnp.float32),
            pltpu.VMEM((8, QB), jnp.float32),
            pltpu.VMEM((STEPS, 8, QB), jnp.float32),
            pltpu.VMEM((8, QB), jnp.float32),
            pltpu.VMEM((8, QB), jnp.float32),
            pltpu.VMEM((8, QB), jnp.float32),
            pltpu.SemaphoreType.DMA((N_PIECES,)),
            pltpu.SemaphoreType.DMA((1,)),
        ],
        compiler_params=pltpu.CompilerParams(vmem_limit_bytes=31 * 1024 * 1024),
        cost_estimate=pl.CostEstimate(flops=8 * 10**9, bytes_accessed=10 * 2**20, transcendentals=5 * 10**6),
    )(at, *pieces, qd)


def pack_kernel(a_ref, b_ref, scale_ref, out_ref):
    scales = jnp.broadcast_to(scale_ref[...].astype(jnp.float32), (TILE, ROWS)).astype(jnp.bfloat16)
    for h in range(HEADS):
        out_ref[h, 0:128, :] = a_ref[0, :, h * HDIM : (h + 1) * HDIM]
        out_ref[h, 128:256, :] = b_ref[0, :, h * HDIM : (h + 1) * HDIM]
        out_ref[h, 256:272, :] = scales


def pack(a, b, scale_ids):
    vmem = pl.BlockSpec(memory_space=pltpu.VMEM)
    return pl.pallas_call(
        pack_kernel,
        out_shape=jax.ShapeDtypeStruct((HEADS, 2 * ROWS + TILE, HDIM), jnp.bfloat16),
        in_specs=[vmem] * 3,
        out_specs=vmem,
    )(a, b, scale_ids)


def unpack_kernel(ad_ref, dkv_ref, attn_ref, dq_ref, dk_ref, dv_ref, buf, sems):
    copies = [pltpu.make_async_copy(ref, buf.at[i], sems.at[i]) for i, ref in enumerate((ad_ref, dkv_ref))]
    for copy in copies:
        copy.start()
    for which, outs in enumerate(((attn_ref, dq_ref), (dk_ref, dv_ref))):
        copies[which].wait()
        for h in range(HEADS):
            for i, out in enumerate(outs):
                tile = buf[which, h, i * ROWS : (i + 1) * ROWS, :]
                if which:
                    tile = tile.astype(jnp.float32).T.astype(jnp.bfloat16)
                out[0, :, h * HDIM : (h + 1) * HDIM] = tile


def unpack(ad, dkv):
    vmem = pl.BlockSpec(memory_space=pltpu.VMEM)
    rows = jax.ShapeDtypeStruct((1, ROWS, HEADS * HDIM), jnp.bfloat16)
    return pl.pallas_call(
        unpack_kernel,
        out_shape=(rows,) * 4,
        in_specs=[pl.BlockSpec(memory_space=pl.ANY)] * 2,
        out_specs=(vmem,) * 4,
        scratch_shapes=[
            pltpu.VMEM((2, HEADS, 2 * ROWS, HDIM), jnp.bfloat16),
            pltpu.SemaphoreType.DMA((2,)),
        ],
    )(ad, dkv)


def add(*arrs):
    total = arrs[0].astype(jnp.float32)
    for arr in arrs[1:]:
        total = total + arr.astype(jnp.float32)
    return total.astype(jnp.bfloat16)


def local(query, key, value, grad_attn, scale_ids):
    def over_heads(arr):
        return lax.all_to_all(arr, "z", split_axis=0, concat_axis=0, tiled=True)

    def right(arr):
        return lax.ppermute(arr, "x", [(i, (i + 1) % XS) for i in range(XS)])

    def left(arr):
        return lax.ppermute(arr, "x", [(i, (i + XS - 1) % XS) for i in range(XS)])

    def swap(arr):
        pairs = [
            (x * ZS + z, (XS - 1 - x if z >= ZS // 2 else x) * ZS + z) for x in range(XS) for z in range(ZS)
        ]
        return lax.ppermute(arr, ("x", "z"), pairs)

    def twin(arr):
        return lax.ppermute(arr, "core", [(0, 1), (1, 0)])

    half = ZS // 2
    at = jnp.stack([lax.axis_index("x"), lax.axis_index("core")]).astype(jnp.int32)

    kvs = over_heads(pack(key, value, scale_ids))
    swapped = swap(pack(query, grad_attn, scale_ids))
    kvs, swapped = lax.optimization_barrier((kvs, swapped))
    from_left, from_right = right(kvs), left(kvs)
    qd = over_heads(swapped)
    opposite_a, opposite_b = right(from_left[:half]), left(from_right[half:])
    pieces = []
    for piece in (kvs, from_left, from_right, opposite_a, opposite_b):
        pieces += [piece, twin(piece)]

    ad, *grads = attention(at, pieces, qd)

    sums = {distance: add(grads[2 * distance], twin(grads[2 * distance + 1])) for distance in (2, 1, 3, 0)}
    right_b, left_a = right(sums[1][half:]), left(sums[3][:half])
    right_a = right(add(sums[1][:half], right(sums[2][:half])))
    left_b = left(add(sums[3][half:], left(sums[2][half:])))
    dkv = jnp.concatenate([add(sums[0][:half], right_a, left_a), add(sums[0][half:], right_b, left_b)], axis=0)
    ad_back = over_heads(ad)
    dkv, ad_back = lax.optimization_barrier((dkv, ad_back))
    return unpack(swap(ad_back), over_heads(dkv))


def solution(mesh):
    fine = Mesh(mesh.devices.reshape(mesh.devices.shape[0], XS, ZS, CS), ("batch", "x", "z", "core"))
    seq = ("x", "z", "core")
    rows = P("batch", seq, None)
    return jax.shard_map(
        local,
        mesh=fine,
        in_specs=(rows, rows, rows, rows, P("batch", seq)),
        out_specs=(rows, rows, rows, rows),
        check_vma=False,
    )
```

```python
import functools

import jax
import jax.numpy as jnp
from jax import lax
from jax.experimental import pallas as pl
from jax.experimental.pallas import tpu as pltpu
from jax.sharding import Mesh, PartitionSpec as P

HEADS = 8
HDIM = 128
ROWS = 128
TILE = 16
XS, ZS, CS = 4, 8, 2
CHUNKS = XS * ZS * CS
QB = 512
KB = 512
SLAB = 256
GROUP = 32
ALL, LATE = slice(0, QB), slice(QB // 2, QB)
STEPS = CHUNKS * ROWS // KB
INV_ROOT = HDIM ** -0.5
LOG2E = 1.4426950408889634
NEG = -1e30

NT = (((1,), (1,)), ((), ()))
TN = (((0,), (0,)), ((), ()))


def dot(a, b, dims=(((1,), (0,)), ((), ()))):
    return lax.dot_general(a, b, dims, preferred_element_type=jnp.float32)


PIECES = ((0, 0, 8), (3, 0, 8), (1, 0, 8), (2, 0, 4), (2, 4, 4))
N_PIECES = 2 * len(PIECES)


def columns(wide):
    return [slice(i, i + SLAB) for i in range(wide.start, wide.stop, SLAB)]


def attention_kernel(at_ref, *refs):
    pieces, qd_in, ad_ref, grads, refs = (
        refs[:N_PIECES], refs[N_PIECES], refs[N_PIECES + 1], refs[N_PIECES + 2 : N_PIECES + 10], refs[N_PIECES + 10 :],
    )
    kvs_ref, qd_ref, s_scr, e_scr, dk_scr, dv_scr, acc_scr, dq_scr, don_scr, dont_scr, q_scr, qt_scr, ds_scr, now_scr, dp_scr, top_scr, tops_scr, delta_scr, sum_scr, qs_scr, sems, qsem = refs
    x, own_core = at_ref[0], at_ref[1]

    def first_chunk(distance, other):
        core = 1 - own_core if other else own_core
        return (lax.rem(x + distance, XS) * CS + core) * ZS

    copies = [pltpu.make_async_copy(qd_in, qd_ref, qsem.at[0])]
    for i, (distance, start, count) in enumerate(PIECES):
        for other in (0, 1):
            n = 2 * i + other
            copies.append(
                pltpu.make_async_copy(
                    pieces[n], kvs_ref.at[pl.ds(first_chunk(distance, other) + start, count)], sems.at[n]
                )
            )
    for copy in copies:
        copy.start()
    dk_scr[...] = jnp.zeros_like(dk_scr)
    dv_scr[...] = jnp.zeros_like(dv_scr)
    for copy in copies:
        copy.wait()

    key_scales = kvs_ref[:, 256:272, :].astype(jnp.float32)[:, 0, :]
    chunk = lax.broadcasted_iota(jnp.int32, key_scales.shape, 0)
    lane = lax.broadcasted_iota(jnp.int32, key_scales.shape, 1)
    core = (chunk // ZS) % CS
    parity = chunk % 2
    is_first = (core == 0) & (parity == 0) & (lane == 0)
    is_last = (core == 1) & (parity == 1) & (lane == ROWS - 1)

    def parts(step):
        base = (step // 4) * 16 + 2 * (step % 4)
        return (base, base + 8)

    def slab(step, half, start):
        return kvs_ref[pl.ds(parts(step)[half], 2), start : start + ROWS, :].reshape(SLAB, HDIM)

    def down(row):
        return jnp.broadcast_to(row, (ROWS, ROWS)).T

    def fold(tile, op):
        return op(tile.reshape(tile.shape[0] // 8, 8, tile.shape[1]), axis=0)

    def one_block(block, _):
        first = block * (QB // ROWS)

        def rows(start):
            return qd_ref[pl.ds(first, QB // ROWS), start : start + ROWS, :].reshape(QB, HDIM)

        own = qd_ref[pl.ds(first, QB // ROWS), 256:272, :].astype(jnp.float32)[:, 0, :]
        for i in range(QB // ROWS):
            qs_scr[:, i * ROWS : (i + 1) * ROWS] = jnp.broadcast_to(own[i : i + 1, :], (8, ROWS))
        late = own[QB // ROWS // 2 :, :]

        def needed(rows):
            return jnp.sum(jnp.where(is_first & (key_scales <= jnp.max(rows)), 1.0, 0.0)).astype(jnp.int32)

        def open_to(rows):
            return jnp.sum(jnp.where(is_last & (key_scales <= jnp.min(rows)), 1.0, 0.0)).astype(jnp.int32)

        n_wide = jnp.maximum(needed(own[: QB // ROWS // 2, :]), 2)
        n_steps = jnp.maximum(needed(late), n_wide)
        n_wide = jnp.where(n_steps - n_wide == 1, n_steps, n_wide)

        def scores(wide, masked, step):
            for half in range(KB // SLAB):
                k = slab(step, half, 0)
                if masked:
                    ks = [
                        down(kvs_ref[parts(step)[half] + i, 256:272, :].astype(jnp.float32)[0:1, :])
                        for i in range(SLAB // ROWS)
                    ]
                for cols in columns(wide):
                    s = dot(k, q_scr[cols, :], NT)
                    for r in range(0, SLAB, GROUP):
                        tile = s[r : r + GROUP, :]
                        if masked:
                            own_ks = ks[r // ROWS][r % ROWS : r % ROWS + GROUP, :]
                            tile = jnp.concatenate(
                                [
                                    jnp.where(
                                        own_ks <= qs_scr[0:1, cols.start + j : cols.start + j + ROWS],
                                        tile[:, j : j + ROWS],
                                        NEG,
                                    )
                                    for j in range(0, SLAB, ROWS)
                                ],
                                axis=1,
                            )
                        s_scr[half * SLAB + r : half * SLAB + r + GROUP, cols] = tile

        q_scr[...] = rows(0)
        qt_scr[...] = rows(0).astype(jnp.float32).T.astype(jnp.bfloat16)
        top_scr[...] = jnp.full_like(top_scr, NEG)
        sum_scr[...] = jnp.zeros_like(sum_scr)
        acc_scr[...] = jnp.zeros_like(acc_scr)

        def weigh(wide, step):
            for half in range(KB // SLAB):
                own = slice(half * SLAB, (half + 1) * SLAB)
                acc_scr[:, wide] += dot(slab(step, half, 128), now_scr[own, wide], TN)

        def exponentials(wide, step):
            top = fold(s_scr[0:GROUP, wide], jnp.max)
            for r in range(GROUP, KB, GROUP):
                top = jnp.maximum(top, fold(s_scr[r : r + GROUP, wide], jnp.max))
            top = jnp.ceil(jnp.max(top, axis=0, keepdims=True) * (INV_ROOT * LOG2E))
            top = jnp.maximum(top_scr[0:1, wide], top)
            drop = jnp.exp2(top_scr[0:1, wide] - top)
            top_scr[:, wide] = jnp.broadcast_to(top, (8, top.shape[1]))
            tops_scr[step, :, wide] = jnp.broadcast_to(top, (8, top.shape[1]))
            acc_scr[:, wide] = acc_scr[:, wide] * drop
            total = sum_scr[:, wide] * drop
            for r in range(0, KB, GROUP):
                e = jnp.exp2(s_scr[r : r + GROUP, wide] * (INV_ROOT * LOG2E) - top)
                total = total + fold(e, jnp.sum)
                e = e.astype(jnp.bfloat16)
                now_scr[r : r + GROUP, wide] = e
                e_scr[step, r : r + GROUP, wide] = e
            sum_scr[:, wide] = total

        def forward(wide, masked, step, _):
            weigh(wide, step - 1)
            exponentials(wide, step)
            scores(wide, masked, step + 1)
            return 0

        def forward_pass(wide, start, n_open, end):
            scores(wide, True, start)
            exponentials(wide, start)
            scores(wide, True, start + 1)
            n_open = jnp.minimum(jnp.maximum(n_open - 1, start + 1), end - 1)
            lax.fori_loop(start + 1, n_open, functools.partial(forward, wide, False), 0)
            lax.fori_loop(n_open, end - 1, functools.partial(forward, wide, True), 0)
            weigh(wide, end - 2)
            exponentials(wide, end - 1)
            weigh(wide, end - 1)

        forward_pass(ALL, 0, open_to(own), n_wide)

        @pl.when(n_steps > n_wide)
        def _():
            forward_pass(LATE, n_wide, open_to(late), n_steps)

        inv = 1.0 / jnp.sum(sum_scr[...], axis=0, keepdims=True)
        attn = (acc_scr[...] * inv).T
        inv_rows = jnp.broadcast_to(inv, (HDIM, QB)).T
        for i in range(QB // ROWS):
            ad_ref[first + i, 0:128, :] = attn[i * ROWS : (i + 1) * ROWS, :].astype(jnp.bfloat16)
        do_n = (rows(128).astype(jnp.float32) * inv_rows).astype(jnp.bfloat16)
        don_scr[...] = do_n
        dont_scr[...] = do_n.astype(jnp.float32).T.astype(jnp.bfloat16)
        delta = jnp.sum(do_n.astype(jnp.float32) * attn, axis=1, keepdims=True)
        delta_scr[...] = jnp.broadcast_to(delta, (QB, HDIM)).T[0:8, :]
        dq_scr[...] = jnp.zeros_like(dq_scr)

        def dprobs(wide, step):
            for half in range(KB // SLAB):
                v = slab(step, half, 128)
                for cols in columns(wide):
                    dp_scr[half * SLAB : (half + 1) * SLAB, cols] = dot(v, don_scr[cols, :], NT)

        def backward(wide, step, _):
            drop = jnp.exp2(tops_scr[step, 0:1, wide] - top_scr[0:1, wide])
            delta = delta_scr[0:1, wide]
            for r in range(0, KB, GROUP):
                e = e_scr[step, r : r + GROUP, wide].astype(jnp.float32) * drop
                now_scr[r : r + GROUP, wide] = e.astype(jnp.bfloat16)
                ds_scr[r : r + GROUP, wide] = (e * (dp_scr[r : r + GROUP, wide] - delta)).astype(jnp.bfloat16)
            for half in range(KB // SLAB):
                dv = dot(dont_scr[:, wide], now_scr[half * SLAB : (half + 1) * SLAB, wide], NT)
                for i in range(SLAB // ROWS):
                    dv_scr[parts(step)[half] + i] += dv[:, i * ROWS : (i + 1) * ROWS]
            dprobs(wide, jnp.minimum(step + 1, STEPS - 1))
            for half in range(KB // SLAB):
                own = slice(half * SLAB, (half + 1) * SLAB)
                dk = dot(qt_scr[:, wide], ds_scr[own, wide], NT)
                for i in range(SLAB // ROWS):
                    dk_scr[parts(step)[half] + i] += dk[:, i * ROWS : (i + 1) * ROWS]
                dq_scr[:, wide] += dot(slab(step, half, 0), ds_scr[own, wide], TN)
            return 0

        def backward_pass(wide, start, end):
            dprobs(wide, start)
            lax.fori_loop(start, end, functools.partial(backward, wide), 0)

        backward_pass(ALL, 0, n_wide)

        @pl.when(n_steps > n_wide)
        def _():
            backward_pass(LATE, n_wide, n_steps)

        dq = (dq_scr[...] * INV_ROOT).T.astype(jnp.bfloat16)
        for i in range(QB // ROWS):
            ad_ref[first + i, 128:256, :] = dq[i * ROWS : (i + 1) * ROWS, :]
        return 0

    lax.fori_loop(0, ZS * ROWS // QB, one_block, 0)

    for distance in range(XS):
        for other in (0, 1):
            out = grads[2 * distance + other]
            base = first_chunk(distance, other)
            out[:, 0:128, :] = (dk_scr[pl.ds(base, ZS)] * INV_ROOT).astype(jnp.bfloat16)
            out[:, 128:256, :] = dv_scr[pl.ds(base, ZS)].astype(jnp.bfloat16)


def attention(at, pieces, qd):
    vmem = pl.BlockSpec(memory_space=pltpu.VMEM)
    outs = (jax.ShapeDtypeStruct((ZS, 2 * ROWS, HDIM), jnp.bfloat16),) * 9
    return pl.pallas_call(
        attention_kernel,
        out_shape=outs,
        in_specs=[pl.BlockSpec(memory_space=pltpu.SMEM)] + [vmem] * (N_PIECES + 1),
        out_specs=(vmem,) * len(outs),
        scratch_shapes=[
            pltpu.VMEM((CHUNKS, 2 * ROWS + TILE, HDIM), jnp.bfloat16),
            pltpu.VMEM((ZS, 2 * ROWS + TILE, HDIM), jnp.bfloat16),
            pltpu.VMEM((KB, QB), jnp.float32),
            pltpu.VMEM((STEPS, KB, QB), jnp.bfloat16),
            pltpu.VMEM((CHUNKS, ROWS, HDIM), jnp.float32),
            pltpu.VMEM((CHUNKS, ROWS, HDIM), jnp.float32),
            pltpu.VMEM((HDIM, QB), jnp.float32),
            pltpu.VMEM((HDIM, QB), jnp.float32),
            pltpu.VMEM((QB, HDIM), jnp.bfloat16),
            pltpu.VMEM((HDIM, QB), jnp.bfloat16),
            pltpu.VMEM((QB, HDIM), jnp.bfloat16),
            pltpu.VMEM((HDIM, QB), jnp.bfloat16),
            pltpu.VMEM((KB, QB), jnp.bfloat16),
            pltpu.VMEM((KB, QB), jnp.bfloat16),
            pltpu.VMEM((KB, QB), jnp.float32),
            pltpu.VMEM((8, QB), jnp.float32),
            pltpu.VMEM((STEPS, 8, QB), jnp.float32),
            pltpu.VMEM((8, QB), jnp.float32),
            pltpu.VMEM((8, QB), jnp.float32),
            pltpu.VMEM((8, QB), jnp.float32),
            pltpu.SemaphoreType.DMA((N_PIECES,)),
            pltpu.SemaphoreType.DMA((1,)),
        ],
        compiler_params=pltpu.CompilerParams(vmem_limit_bytes=34 * 1024 * 1024),
        cost_estimate=pl.CostEstimate(flops=8 * 10**9, bytes_accessed=10 * 2**20, transcendentals=5 * 10**6),
    )(at, *pieces, qd)


def pack_kernel(a_ref, b_ref, scale_ref, out_ref):
    scales = jnp.broadcast_to(scale_ref[...].astype(jnp.float32), (TILE, ROWS)).astype(jnp.bfloat16)
    for h in range(HEADS):
        out_ref[h, 0:128, :] = a_ref[0, :, h * HDIM : (h + 1) * HDIM]
        out_ref[h, 128:256, :] = b_ref[0, :, h * HDIM : (h + 1) * HDIM]
        out_ref[h, 256:272, :] = scales


def pack(a, b, scale_ids):
    vmem = pl.BlockSpec(memory_space=pltpu.VMEM)
    return pl.pallas_call(
        pack_kernel,
        out_shape=jax.ShapeDtypeStruct((HEADS, 2 * ROWS + TILE, HDIM), jnp.bfloat16),
        in_specs=[vmem] * 3,
        out_specs=vmem,
    )(a, b, scale_ids)


def unpack_kernel(ad_ref, dkv_ref, attn_ref, dq_ref, dk_ref, dv_ref, buf, sems):
    copies = [pltpu.make_async_copy(ref, buf.at[i], sems.at[i]) for i, ref in enumerate((ad_ref, dkv_ref))]
    for copy in copies:
        copy.start()
    for which, outs in enumerate(((attn_ref, dq_ref), (dk_ref, dv_ref))):
        copies[which].wait()
        for h in range(HEADS):
            for i, out in enumerate(outs):
                tile = buf[which, h, i * ROWS : (i + 1) * ROWS, :]
                if which:
                    tile = tile.astype(jnp.float32).T.astype(jnp.bfloat16)
                out[0, :, h * HDIM : (h + 1) * HDIM] = tile


def unpack(ad, dkv):
    vmem = pl.BlockSpec(memory_space=pltpu.VMEM)
    rows = jax.ShapeDtypeStruct((1, ROWS, HEADS * HDIM), jnp.bfloat16)
    return pl.pallas_call(
        unpack_kernel,
        out_shape=(rows,) * 4,
        in_specs=[pl.BlockSpec(memory_space=pl.ANY)] * 2,
        out_specs=(vmem,) * 4,
        scratch_shapes=[
            pltpu.VMEM((2, HEADS, 2 * ROWS, HDIM), jnp.bfloat16),
            pltpu.SemaphoreType.DMA((2,)),
        ],
    )(ad, dkv)


def add(*arrs):
    total = arrs[0].astype(jnp.float32)
    for arr in arrs[1:]:
        total = total + arr.astype(jnp.float32)
    return total.astype(jnp.bfloat16)


def local(query, key, value, grad_attn, scale_ids):
    def over_heads(arr):
        return lax.all_to_all(arr, "z", split_axis=0, concat_axis=0, tiled=True)

    def right(arr):
        return lax.ppermute(arr, "x", [(i, (i + 1) % XS) for i in range(XS)])

    def left(arr):
        return lax.ppermute(arr, "x", [(i, (i + XS - 1) % XS) for i in range(XS)])

    def swap(arr):
        pairs = [
            (x * ZS + z, (XS - 1 - x if z >= ZS // 2 else x) * ZS + z) for x in range(XS) for z in range(ZS)
        ]
        return lax.ppermute(arr, ("x", "z"), pairs)

    def twin(arr):
        return lax.ppermute(arr, "core", [(0, 1), (1, 0)])

    half = ZS // 2
    at = jnp.stack([lax.axis_index("x"), lax.axis_index("core")]).astype(jnp.int32)

    kvs = over_heads(pack(key, value, scale_ids))
    swapped = swap(pack(query, grad_attn, scale_ids))
    kvs, swapped = lax.optimization_barrier((kvs, swapped))
    from_left, from_right = right(kvs), left(kvs)
    qd = over_heads(swapped)
    opposite_a, opposite_b = right(from_left[:half]), left(from_right[half:])
    pieces = []
    for piece in (kvs, from_left, from_right, opposite_a, opposite_b):
        pieces += [piece, twin(piece)]

    ad, *grads = attention(at, pieces, qd)

    far = add(grads[4], twin(grads[5]))
    far, *grads = lax.optimization_barrier((far, *grads))
    sums = {distance: add(grads[2 * distance], twin(grads[2 * distance + 1])) for distance in (3, 1, 0)}
    k, v = slice(0, ROWS), slice(ROWS, 2 * ROWS)
    key_left = left(sums[3][:, k])
    key_relay = add(sums[1][:, k], right(far[:, k]))
    value_relay = add(sums[3][:, v], left(far[:, v]))
    ad, key_relay, value_relay = lax.optimization_barrier((ad, key_relay, value_relay))
    ad_back = over_heads(ad)
    key_right, value_left = right(key_relay), left(value_relay)
    value_right = right(sums[1][:, v])
    key_sum = add(sums[0][:, k], key_right, key_left)
    value_sum = add(sums[0][:, v], value_right, value_left)
    sums = jnp.concatenate([key_sum, value_sum], axis=1)
    sums, ad_back = lax.optimization_barrier((sums, ad_back))
    return unpack(swap(ad_back), over_heads(sums))


def solution(mesh):
    fine = Mesh(mesh.devices.reshape(mesh.devices.shape[0], XS, ZS, CS), ("batch", "x", "z", "core"))
    seq = ("x", "z", "core")
    rows = P("batch", seq, None)
    return jax.shard_map(
        local,
        mesh=fine,
        in_specs=(rows, rows, rows, rows, P("batch", seq)),
        out_specs=(rows, rows, rows, rows),
        check_vma=False,
    )
```
